32 devices in a mesh: users: 8 (over y, x, core), items: 4 (over z).
Axes of the slice: x: 2, y: 2, z: 4, core: 2. Of those that a mesh axis runs over, the one named last changes fastest.
Arguments:
- user_factors: float32 [16384, 128], P('users'), may hold values from -1.8 to 1.8
- user_moment_one: float32 [16384, 128], P('users'), may hold values from -1.8 to 1.8
- user_moment_two: float32 [16384, 128], P('users'), may hold values from 0.01 to 1
- item_factors: float32 [6144, 128], P(('items', 'users')), may hold values from -1.8 to 1.8
- item_moment_one: float32 [6144, 128], P(('items', 'users')), may hold values from -1.8 to 1.8
- item_moment_two: float32 [6144, 128], P(('items', 'users')), may hold values from 0.01 to 1
- block_slot: int32 [8, 4, 128], P('users', 'items'), may hold values from 0 to 191, as said below
- block_count: int32 [8, 4], P('users', 'items'), may hold values from 32 to 128, as said below
- block_values: bfloat16 [8, 4, 128, 128, 128], P('users', 'items'), may hold values from 0 to 4
Outputs:
- new_user_factors: float32 [16384, 128], P(('users', 'items'))
- new_user_moment_one: float32 [16384, 128], P(('users', 'items'))
- new_user_moment_two: float32 [16384, 128], P(('users', 'items'))
- new_item_factors: float32 [6144, 128], P(('items', 'users'))
- new_item_moment_one: float32 [6144, 128], P(('items', 'users'))
- new_item_moment_two: float32 [6144, 128], P(('items', 'users'))
The draws below stay inside these ranges and needn't reach their ends.
Inputs may be any that keep to these rules, and one draw needn't show every extreme that they name: `block_slot`: in every grid cell the 128 entries are distinct. `block_count`: some grid cell has exactly 128 live blocks.
All inputs are finite; a program needn't handle non-finite values.
Results may differ from the reference program's by a relative error of at most 0.0046.
Values may be sent and summed in bfloat16 or wider, within the bound.
A program may use at most 64 MiB of HBM per device.

```python
import math
import jax
import jax.numpy as jnp
from jax import lax

R = 128
BS = 128
UBLK = 16
IBLK = 12
MAXB = 128
GRID_ROWS = 8
GRID_COLS = 4
NU = 16384
NI = 6144


def draw_block_slot(key, part):
    cell_keys = jax.random.split(jax.random.fold_in(key, 11), GRID_ROWS * GRID_COLS)
    orderings = jax.vmap(lambda single: jax.random.permutation(single, UBLK * IBLK)[:MAXB])(cell_keys)
    return orderings.reshape(GRID_ROWS, GRID_COLS, MAXB).astype(jnp.int32)


def draw_block_count(key, part):
    cell_total = GRID_ROWS * GRID_COLS
    divider = jax.random.randint(jax.random.fold_in(key, 23), (cell_total,), 1, 5)
    counts = MAXB // divider
    chosen = jax.random.randint(jax.random.fold_in(key, 29), (), 0, cell_total)
    counts = jnp.where(jnp.arange(cell_total) == chosen, MAXB, counts)
    return counts.reshape(GRID_ROWS, GRID_COLS).astype(jnp.int32)


def levels(rng, extent, pieces, smallest, top_value):
    def one(position, shards_of):
        steps = jax.random.uniform(jax.random.fold_in(jax.random.fold_in(rng, 6), position), (shards_of,), jnp.float32, smallest / len(pieces), top_value / len(pieces))
        return jnp.repeat(jnp.exp(steps), extent[position] // shards_of).reshape((-1,) + (1,) * (len(extent) - position - 1))

    loudness = one(*pieces[0])
    for cut in pieces[1:]:
        loudness = loudness * one(*cut)
    return loudness


def noise(key, extent, width, bound, cuts=(), held_as=jnp.bfloat16):
    drawn = width * jax.random.normal(key, extent, jnp.float32)
    if cuts:
        drawn = drawn * levels(key, extent, cuts, -0.22, 0.18)
    return jnp.clip(drawn, -bound, bound).astype(held_as)


def setup_inputs(seed: int = 0) -> dict:
    keys = jax.random.split(jax.random.key(seed), 10)
    return {
        "user_factors": noise(keys[0], (NU, R), 0.3, 1.8, ((0, 8),), jnp.float32),
        "user_moment_one": noise(keys[1], (NU, R), 0.3, 1.8, ((0, 8),), jnp.float32),
        "user_moment_two": jnp.clip(jnp.exp(math.log(1.0) - 4.6051702 * jax.random.uniform(keys[2], (NU, R), jnp.float32) ** levels(keys[2], (NU, R), ((0, 8),), -0.2, 0.2)), 0.01, 1.0),
        "item_factors": noise(keys[3], (NI, R), 0.3, 1.8, ((0, 32),), jnp.float32),
        "item_moment_one": noise(keys[4], (NI, R), 0.3, 1.8, ((0, 32),), jnp.float32),
        "item_moment_two": jnp.clip(jnp.exp(math.log(1.0) - 4.6051702 * jax.random.uniform(keys[5], (NI, R), jnp.float32) ** levels(keys[5], (NI, R), ((0, 32),), -0.2, 0.2)), 0.01, 1.0),
        "block_slot": draw_block_slot(jax.random.fold_in(keys[9], 71), 0),
        "block_count": draw_block_count(jax.random.fold_in(keys[9], 71), 0),
        "block_values": jnp.clip(4.0 * jax.random.uniform(keys[8], (GRID_ROWS, GRID_COLS, MAXB, BS, BS), jnp.float32) ** levels(keys[8], (GRID_ROWS, GRID_COLS, MAXB, BS, BS), ((0, 8), (1, 4)), -0.2, 0.2), 0.0, 4.0).astype(jnp.bfloat16),
    }


conf_alpha = 0.5
reg_weight = 0.5
beta_one = 0.9
beta_two = 0.95
learn_rate = 0.1
adam_eps = 1e-08
correction_one = 1.0 - beta_one ** 11
correction_two = 1.0 - beta_two ** 11

def adam_update(parameter, first_moment, second_moment, grad_sum, grad_scale):
    gradient = grad_sum * grad_scale + reg_weight * parameter
    first_new = beta_one * first_moment + (1.0 - beta_one) * gradient
    second_new = beta_two * second_moment + (1.0 - beta_two) * gradient * gradient
    step_size = first_new / correction_one / (jnp.sqrt(second_new / correction_two) + adam_eps)
    return (parameter - learn_rate * step_size, first_new, second_new)

def weighted_error(predicted, block_vals, live_mask):
    target = block_vals.astype(jnp.float32)
    return jnp.where(live_mask, (1.0 + conf_alpha * target) * (predicted - target), 0.0).astype(jnp.bfloat16)

def cell_error(user_tiles, item_tiles, block_slot, block_count, block_values, row_index, col_index):
    slot_list = block_slot[row_index, col_index]
    live_mask = jnp.arange(MAXB, dtype=jnp.int32) < block_count[row_index, col_index]
    user_part = (slot_list // IBLK).astype(jnp.int32)
    item_part = (slot_list % IBLK).astype(jnp.int32)
    user_rows = user_tiles[row_index][user_part].astype(jnp.float32)
    item_rows = item_tiles[col_index][item_part].astype(jnp.float32)
    predicted = jnp.einsum('kar,kbr->kab', user_rows, item_rows)
    weighted = weighted_error(predicted, block_values[row_index, col_index], live_mask[:, None, None])
    weighted = lax.optimization_barrier(weighted).astype(jnp.float32)
    return (weighted, user_part, item_part, user_rows, item_rows)

def user_pass(user_low, item_low, block_slot, block_count, block_values):
    user_tiles = lax.optimization_barrier(user_low).reshape(GRID_ROWS, UBLK, BS, R)
    item_tiles = lax.optimization_barrier(item_low).reshape(GRID_COLS, IBLK, BS, R)

    def one_row(row_index):

        def one_cell(running, col_index):
            weighted, user_part, item_part, user_rows, item_rows = cell_error(user_tiles, item_tiles, block_slot, block_count, block_values, row_index, col_index)
            running = running.at[user_part].add(jnp.einsum('kab,kbr->kar', weighted, item_rows))
            return (running, None)
        running, _ = lax.scan(one_cell, jnp.zeros((UBLK, BS, R), jnp.float32), jnp.arange(GRID_COLS, dtype=jnp.int32))
        return running
    return lax.map(one_row, jnp.arange(GRID_ROWS, dtype=jnp.int32)).reshape(NU, R)

def item_pass(user_low, item_low, block_slot, block_count, block_values):
    user_tiles = lax.optimization_barrier(user_low).reshape(GRID_ROWS, UBLK, BS, R)
    item_tiles = lax.optimization_barrier(item_low).reshape(GRID_COLS, IBLK, BS, R)

    def one_col(col_index):

        def one_cell(running, row_index):
            weighted, user_part, item_part, user_rows, item_rows = cell_error(user_tiles, item_tiles, block_slot, block_count, block_values, row_index, col_index)
            running = running.at[item_part].add(jnp.einsum('kab,kar->kbr', weighted, user_rows))
            return (running, None)
        running, _ = lax.scan(one_cell, jnp.zeros((IBLK, BS, R), jnp.float32), jnp.arange(GRID_ROWS, dtype=jnp.int32))
        return running
    return lax.map(one_col, jnp.arange(GRID_COLS, dtype=jnp.int32)).reshape(NI, R)

def reference(user_factors, user_moment_one, user_moment_two, item_factors, item_moment_one, item_moment_two, block_slot, block_count, block_values):
    item_low = item_factors.astype(jnp.bfloat16)
    user_low = user_factors.astype(jnp.bfloat16)
    user_sum = user_pass(user_low, item_low, block_slot, block_count, block_values)
    new_user, new_user_one, new_user_two = adam_update(user_factors, user_moment_one, user_moment_two, user_sum, 1.0 / math.sqrt(NI))
    new_user_low = new_user.astype(jnp.bfloat16)
    item_sum = item_pass(new_user_low, item_low, block_slot, block_count, block_values)
    new_item, new_item_one, new_item_two = adam_update(item_factors, item_moment_one, item_moment_two, item_sum, 1.0 / math.sqrt(NU))
    return (new_user, new_user_one, new_user_two, new_item, new_item_one, new_item_two)
```

```python
import functools
import math

import jax
import jax.numpy as jnp
from jax import lax
from jax.experimental import pallas as pl
from jax.experimental.pallas import tpu as pltpu
from jax.sharding import PartitionSpec as P

conf_alpha = 0.5
reg_weight = 0.5
beta_one = 0.9
beta_two = 0.95
learn_rate = 0.1
adam_eps = 1e-08
correction_one = 1.0 - beta_one**11
correction_two = 1.0 - beta_two**11

f32, bf16 = jnp.float32, jnp.bfloat16


def adam_update(parameter, first_moment, second_moment, grad_sum, grad_scale):
    gradient = grad_sum * grad_scale + reg_weight * parameter
    first_new = beta_one * first_moment + (1.0 - beta_one) * gradient
    second_new = beta_two * second_moment + (1.0 - beta_two) * gradient * gradient
    step_size = first_new / correction_one / (jnp.sqrt(second_new / correction_two) + adam_eps)
    return (parameter - learn_rate * step_size, first_new, second_new)


def find_blocks(slot_list, live_count, slots):
    places = jnp.arange(slot_list.shape[0], dtype=jnp.int32)
    here = (slot_list[None, :] == jnp.arange(slots, dtype=jnp.int32)[:, None]) & (
        places < live_count
    )[None, :]
    return jnp.max(jnp.where(here, places[None, :], -1), axis=1)


def kernel(
    n_users, n_items, edge,
    place, uf_hbm, um1_hbm, um2_hbm, if_hbm, im1_hbm, im2_hbm, vals_hbm,
    nu_hbm, nu1_hbm, nu2_hbm, ni_hbm, ni1_hbm, ni2_hbm,
    vals, uf, um1, um2, itf, im1, im2, u_low, panel, item_t,
    acc, send_u, recv_u, new_low, item_acc, item_sum, item_send, recv_i,
    load_sem, store_sem, gs_sem, gr_sem, us_sem, ur_sem, as_sem, ar_sem, is_sem, ir_sem,
):
    me_u, me_i = lax.axis_index("users"), lax.axis_index("items")
    user_rows, rank = uf.shape
    item_rows = panel.shape[0]
    user_share, item_share = user_rows // n_items, item_rows // n_users
    share_blocks, item_blocks = user_share // edge, item_rows // edge
    width = 2 if item_blocks % 2 == 0 else 1
    pairs = item_blocks // width
    span = width * edge

    def u_share(j):
        return pl.ds(pl.multiple_of(j * user_share, user_share), user_share)

    def i_share(j):
        return pl.ds(pl.multiple_of(j * item_share, item_share), item_share)

    def to(src, dst, s_sem, r_sem, axis, j):
        return pltpu.make_async_remote_copy(
            src_ref=src, dst_ref=dst, send_sem=s_sem, recv_sem=r_sem,
            device_id={axis: j}, device_id_type=pl.DeviceIdType.MESH,
        )

    def user_peers(body):
        def step(t, carry):
            body(lax.rem(me_u + t, n_users))
            return carry

        lax.fori_loop(1, n_users, step, 0)

    def item_peers(body):
        def step(t, carry):
            body(lax.rem(me_i + t, n_items))
            return carry

        lax.fori_loop(1, n_items, step, 0)

    own = u_share(me_i)
    loads = [
        pltpu.make_async_copy(src, dst, load_sem.at[n])
        for n, (src, dst) in enumerate(
            (
                (if_hbm, itf), (uf_hbm, uf), (vals_hbm, vals),
                (um1_hbm.at[own], um1), (um2_hbm.at[own], um2),
                (im1_hbm, im1), (im2_hbm, im2),
            )
        )
    ]
    for load in loads:
        load.start()

    barrier = pltpu.get_barrier_semaphore()

    def greet_user(j):
        pl.semaphore_signal(
            barrier, inc=1, device_id={"users": j}, device_id_type=pl.DeviceIdType.MESH
        )

    def greet_item(j):
        pl.semaphore_signal(
            barrier, inc=1, device_id={"items": j}, device_id_type=pl.DeviceIdType.MESH
        )

    user_peers(greet_user)
    item_peers(greet_item)
    loads[0].wait()
    panel[i_share(me_u), :] = itf[...].astype(bf16)
    pl.semaphore_wait(barrier, n_users + n_items - 2)

    def gather(j):
        mine = panel.at[i_share(me_u)]
        return to(mine, mine, gs_sem.at[j], gr_sem.at[me_u], "users", j)

    def gathered(j):
        theirs = panel.at[i_share(j)]
        return to(theirs, theirs, gs_sem.at[j], gr_sem.at[j], "users", j)

    user_peers(lambda j: gather(j).start())
    loads[1].wait()
    u_low[...] = uf[...].astype(bf16)
    loads[2].wait()
    user_peers(lambda j: gathered(j).wait_recv())
    for b in range(item_blocks):
        item_t[:, b * edge : (b + 1) * edge] = panel[b * edge : (b + 1) * edge, :].T

    def errors(rows, first_block, p):
        cols = item_t[:, pl.ds(pl.multiple_of(p * span, span), span)]
        predicted = jnp.dot(rows, cols, preferred_element_type=f32)
        strips = []
        for ub in range(share_blocks):
            parts = []
            for h in range(width):
                k = place[(first_block + ub) * item_blocks + p * width + h]
                live = jnp.where(k < 0, 0.0, 1.0).astype(f32)
                y = vals[jnp.maximum(k, 0)].astype(f32)
                pred = predicted[ub * edge : (ub + 1) * edge, h * edge : (h + 1) * edge]
                parts.append(((live + (conf_alpha * live) * y) * (pred - y)).astype(bf16))
            strips.append(jnp.concatenate(parts, axis=1))
        return jnp.concatenate(strips, axis=0)

    def send_share(j):
        return to(send_u.at[j], recv_u.at[me_i], us_sem.at[j], ur_sem.at[me_i], "items", j)

    def first_pass(t, carry):
        j = lax.rem(me_i + 1 + t, n_items)
        acc[...] = jnp.zeros_like(acc)

        def step(p, c):
            rows = u_low[u_share(j), :]
            weighted = errors(rows, j * share_blocks, p)
            it = panel[pl.ds(pl.multiple_of(p * span, span), span), :]
            acc[...] += jnp.dot(weighted, it, preferred_element_type=f32)
            return c

        lax.fori_loop(0, pairs, step, 0)

        @pl.when(t < n_items - 1)
        def _():
            send_u[j] = acc[...].astype(bf16)
            send_share(j).start()

        return carry

    lax.fori_loop(0, n_items, first_pass, 0)
    loads[3].wait()
    loads[4].wait()

    def add_share(j):
        to(
            send_u.at[j], recv_u.at[j], us_sem.at[j], ur_sem.at[j], "items", j
        ).wait_recv()
        acc[...] += recv_u[j].astype(f32)

    item_peers(add_share)
    user_scale = 1.0 / math.sqrt(item_rows * n_items)
    new, one, two = adam_update(uf[own, :], um1[...], um2[...], acc[...], user_scale)
    new_low[own, :] = new.astype(bf16)

    def spread(j):
        mine = new_low.at[own]
        return to(mine, mine, as_sem.at[j], ar_sem.at[me_i], "items", j)

    item_peers(lambda j: spread(j).start())
    acc[...] = new
    um1[...] = one
    um2[...] = two
    stores = [
        pltpu.make_async_copy(src, dst, store_sem.at[n])
        for n, (src, dst) in enumerate(
            (
                (acc, nu_hbm), (um1, nu1_hbm), (um2, nu2_hbm),
                (itf, ni_hbm), (im1, ni1_hbm), (im2, ni2_hbm),
            )
        )
    ]
    for store in stores[:3]:
        store.start()

    item_acc[...] = jnp.zeros_like(item_acc)

    def second_pass(t, carry):
        j = lax.rem(me_i + t, n_items)

        @pl.when(t > 0)
        def _():
            theirs = new_low.at[u_share(j)]
            to(theirs, theirs, as_sem.at[j], ar_sem.at[j], "items", j).wait_recv()

        rows_t = jnp.concatenate(
            [
                new_low[pl.ds(pl.multiple_of((j * share_blocks + b) * edge, edge), edge), :].T
                for b in range(share_blocks)
            ],
            axis=1,
        )

        def step(p, c):
            rows = new_low[u_share(j), :]
            weighted = errors(rows, j * share_blocks, p)
            cols = pl.ds(pl.multiple_of(p * span, span), span)
            item_acc[:, cols] += jnp.dot(rows_t, weighted, preferred_element_type=f32)
            return c

        lax.fori_loop(0, pairs, step, 0)
        return carry

    lax.fori_loop(0, n_items, second_pass, 0)
    for b in range(item_blocks):
        tile = item_acc[:, b * edge : (b + 1) * edge].T
        item_sum[b * edge : (b + 1) * edge, :] = tile
        item_send[b * edge : (b + 1) * edge, :] = tile.astype(bf16)

    def send_items(j):
        return to(
            item_send.at[i_share(j)], recv_i.at[me_u],
            is_sem.at[j], ir_sem.at[me_u], "users", j,
        )

    user_peers(lambda j: send_items(j).start())
    loads[5].wait()
    loads[6].wait()

    def add_items(j):
        to(
            item_send.at[i_share(j)], recv_i.at[j], is_sem.at[j], ir_sem.at[j], "users", j
        ).wait_recv()
        item_sum[i_share(me_u), :] += recv_i[j].astype(f32)

    user_peers(add_items)
    item_scale = 1.0 / math.sqrt(user_rows * n_users)
    new, one, two = adam_update(
        itf[...], im1[...], im2[...], item_sum[i_share(me_u), :], item_scale
    )
    itf[...] = new
    im1[...] = one
    im2[...] = two
    for store in stores[3:]:
        store.start()

    user_peers(lambda j: gather(j).wait_send())
    user_peers(lambda j: send_items(j).wait_send())
    item_peers(lambda j: send_share(j).wait_send())
    item_peers(lambda j: spread(j).wait_send())
    for store in stores:
        store.wait()


def on_device(
    n_users, n_items,
    user_factors, user_moment_one, user_moment_two,
    item_factors, item_moment_one, item_moment_two,
    block_slot, block_count, block_values,
):
    values = block_values[0, 0]
    edge = values.shape[-1]
    user_rows, rank = user_factors.shape
    item_share = item_factors.shape[0]
    item_rows = item_share * n_users
    user_share = user_rows // n_items
    slots = (user_rows // edge) * (item_rows // edge)
    place = find_blocks(block_slot[0, 0], block_count[0, 0], slots)
    vm = pltpu.VMEM
    dma = pltpu.SemaphoreType.DMA
    user_out = jax.ShapeDtypeStruct((user_share, rank), f32)
    item_out = jax.ShapeDtypeStruct((item_share, rank), f32)
    anywhere = pl.BlockSpec(memory_space=pl.ANY)
    return pl.pallas_call(
        functools.partial(kernel, n_users, n_items, edge),
        out_shape=(user_out,) * 3 + (item_out,) * 3,
        in_specs=[pl.BlockSpec(memory_space=pltpu.SMEM)] + [anywhere] * 7,
        out_specs=(anywhere,) * 6,
        scratch_shapes=[
            vm(values.shape, bf16),
            vm((user_rows, rank), f32),
            vm((user_share, rank), f32),
            vm((user_share, rank), f32),
            vm((item_share, rank), f32),
            vm((item_share, rank), f32),
            vm((item_share, rank), f32),
            vm((user_rows, rank), bf16),
            vm((item_rows, rank), bf16),
            vm((rank, item_rows), bf16),
            vm((user_share, rank), f32),
            vm((n_items, user_share, rank), bf16),
            vm((n_items, user_share, rank), bf16),
            vm((user_rows, rank), bf16),
            vm((rank, item_rows), f32),
            vm((item_rows, rank), f32),
            vm((item_rows, rank), bf16),
            vm((n_users, item_share, rank), bf16),
            dma((7,)),
            dma((6,)),
            dma((n_users,)),
            dma((n_users,)),
            dma((n_items,)),
            dma((n_items,)),
            dma((n_items,)),
            dma((n_items,)),
            dma((n_users,)),
            dma((n_users,)),
        ],
        compiler_params=pltpu.CompilerParams(
            collective_id=0, has_side_effects=True, vmem_limit_bytes=56 * 2**20
        ),
        name="factorization_step",
    )(
        place, user_factors, user_moment_one, user_moment_two,
        item_factors, item_moment_one, item_moment_two, values,
    )


def solution(mesh):
    return jax.shard_map(
        functools.partial(on_device, mesh.shape["users"], mesh.shape["items"]),
        mesh=mesh,
        in_specs=(
            P("users", None),
            P("users", None),
            P("users", None),
            P(("items", "users"), None),
            P(("items", "users"), None),
            P(("items", "users"), None),
            P("users", "items", None),
            P("users", "items"),
            P("users", "items", None, None, None),
        ),
        out_specs=(
            P(("users", "items"), None),
            P(("users", "items"), None),
            P(("users", "items"), None),
            P(("items", "users"), None),
            P(("items", "users"), None),
            P(("items", "users"), None),
        ),
        check_vma=False,
    )
```

```python
import functools
import math

import jax
import jax.numpy as jnp
from jax import lax
from jax.experimental import pallas as pl
from jax.experimental.pallas import tpu as pltpu
from jax.sharding import PartitionSpec as P

conf_alpha = 0.5
reg_weight = 0.5
beta_one = 0.9
beta_two = 0.95
learn_rate = 0.1
adam_eps = 1e-08
correction_one = 1.0 - beta_one**11
correction_two = 1.0 - beta_two**11

f32, bf16 = jnp.float32, jnp.bfloat16


def adam_update(parameter, first_moment, second_moment, grad_sum, grad_scale):
    gradient = grad_sum * grad_scale + reg_weight * parameter
    first_new = beta_one * first_moment + (1.0 - beta_one) * gradient
    second_new = beta_two * second_moment + (1.0 - beta_two) * gradient * gradient
    step_size = first_new / correction_one / (jnp.sqrt(second_new / correction_two) + adam_eps)
    return (parameter - learn_rate * step_size, first_new, second_new)


def find_blocks(slot_list, live_count, slots):
    places = jnp.arange(slot_list.shape[0], dtype=jnp.int32)
    here = (slot_list[None, :] == jnp.arange(slots, dtype=jnp.int32)[:, None]) & (
        places < live_count
    )[None, :]
    return jnp.max(jnp.where(here, places[None, :], -1), axis=1)


def kernel(
    n_users, n_items, edge,
    place, uf_hbm, um1_hbm, um2_hbm, if_hbm, im1_hbm, im2_hbm, vals_hbm,
    nu_hbm, nu1_hbm, nu2_hbm, ni_hbm, ni1_hbm, ni2_hbm,
    vals, uf, um1, um2, itf, im1, im2, u_low, panel, item_t,
    acc, send_u, recv_u, new_low, item_acc, item_sum, item_send, recv_i,
    load_sem, store_sem, gs_sem, gr_sem, us_sem, ur_sem, as_sem, ar_sem, is_sem, ir_sem,
):
    me_u, me_i = lax.axis_index("users"), lax.axis_index("items")
    user_rows, rank = uf.shape
    item_rows = panel.shape[0]
    user_share, item_share = user_rows // n_items, item_rows // n_users
    share_blocks, item_blocks = user_share // edge, item_rows // edge
    width = 2 if item_blocks % 2 == 0 else 1
    pairs = item_blocks // width
    span = width * edge

    def u_share(j):
        return pl.ds(pl.multiple_of(j * user_share, user_share), user_share)

    def i_share(j):
        return pl.ds(pl.multiple_of(j * item_share, item_share), item_share)

    def to(src, dst, s_sem, r_sem, axis, j):
        return pltpu.make_async_remote_copy(
            src_ref=src, dst_ref=dst, send_sem=s_sem, recv_sem=r_sem,
            device_id={axis: j}, device_id_type=pl.DeviceIdType.MESH,
        )

    def user_peers(body):
        def step(t, carry):
            body(lax.rem(me_u + t, n_users))
            return carry

        lax.fori_loop(1, n_users, step, 0)

    def item_peers(body):
        def step(t, carry):
            body(lax.rem(me_i + t, n_items))
            return carry

        lax.fori_loop(1, n_items, step, 0)

    own = u_share(me_i)
    loads = [
        pltpu.make_async_copy(src, dst, load_sem.at[n])
        for n, (src, dst) in enumerate(
            (
                (if_hbm, itf), (uf_hbm, uf), (vals_hbm, vals),
                (um1_hbm.at[own], um1), (um2_hbm.at[own], um2),
                (im1_hbm, im1), (im2_hbm, im2),
            )
        )
    ]
    for load in loads:
        load.start()

    barrier = pltpu.get_barrier_semaphore()

    def greet_user(j):
        pl.semaphore_signal(
            barrier, inc=1, device_id={"users": j}, device_id_type=pl.DeviceIdType.MESH
        )

    def greet_item(j):
        pl.semaphore_signal(
            barrier, inc=1, device_id={"items": j}, device_id_type=pl.DeviceIdType.MESH
        )

    user_peers(greet_user)
    item_peers(greet_item)
    loads[0].wait()
    panel[i_share(me_u), :] = itf[...].astype(bf16)
    pl.semaphore_wait(barrier, n_users + n_items - 2)

    def gather(j):
        mine = panel.at[i_share(me_u)]
        return to(mine, mine, gs_sem.at[j], gr_sem.at[me_u], "users", j)

    def gathered(j):
        theirs = panel.at[i_share(j)]
        return to(theirs, theirs, gs_sem.at[j], gr_sem.at[j], "users", j)

    user_peers(lambda j: gather(j).start())
    loads[1].wait()
    u_low[...] = uf[...].astype(bf16)
    loads[2].wait()
    user_peers(lambda j: gathered(j).wait_recv())
    for b in range(item_blocks):
        item_t[:, b * edge : (b + 1) * edge] = panel[b * edge : (b + 1) * edge, :].T

    def errors(rows, first_block, p):
        cols = item_t[:, pl.ds(pl.multiple_of(p * span, span), span)]
        predicted = jnp.dot(rows, cols, preferred_element_type=f32)
        strips = []
        for ub in range(share_blocks):
            parts = []
            for h in range(width):
                k = place[(first_block + ub) * item_blocks + p * width + h]
                live = jnp.where(k < 0, 0.0, 1.0).astype(f32)
                y = vals[jnp.maximum(k, 0)].astype(f32)
                pred = predicted[ub * edge : (ub + 1) * edge, h * edge : (h + 1) * edge]
                parts.append(((live + (conf_alpha * live) * y) * (pred - y)).astype(bf16))
            strips.append(jnp.concatenate(parts, axis=1))
        return jnp.concatenate(strips, axis=0)

    def send_share(j):
        return to(send_u.at[j], recv_u.at[me_i], us_sem.at[j], ur_sem.at[me_i], "items", j)

    def first_pass(t, carry):
        j = lax.rem(me_i + 1 + t, n_items)
        acc[...] = jnp.zeros_like(acc)

        def step(p, c):
            rows = u_low[u_share(j), :]
            weighted = errors(rows, j * share_blocks, p)
            it = panel[pl.ds(pl.multiple_of(p * span, span), span), :]
            acc[...] += jnp.dot(weighted, it, preferred_element_type=f32)
            return c

        lax.fori_loop(0, pairs, step, 0)

        @pl.when(t < n_items - 1)
        def _():
            send_u[j] = acc[...].astype(bf16)
            send_share(j).start()

        return carry

    lax.fori_loop(0, n_items, first_pass, 0)
    loads[3].wait()
    loads[4].wait()

    def add_share(j):
        to(
            send_u.at[j], recv_u.at[j], us_sem.at[j], ur_sem.at[j], "items", j
        ).wait_recv()
        acc[...] += recv_u[j].astype(f32)

    item_peers(add_share)
    user_scale = 1.0 / math.sqrt(item_rows * n_items)
    new, one, two = adam_update(uf[own, :], um1[...], um2[...], acc[...], user_scale)
    new_low[own, :] = new.astype(bf16)

    def spread(j):
        mine = new_low.at[own]
        return to(mine, mine, as_sem.at[j], ar_sem.at[me_i], "items", j)

    item_peers(lambda j: spread(j).start())
    acc[...] = new
    um1[...] = one
    um2[...] = two
    stores = [
        pltpu.make_async_copy(src, dst, store_sem.at[n])
        for n, (src, dst) in enumerate(
            (
                (acc, nu_hbm), (um1, nu1_hbm), (um2, nu2_hbm),
                (itf, ni_hbm), (im1, ni1_hbm), (im2, ni2_hbm),
            )
        )
    ]
    for store in stores[:3]:
        store.start()

    item_acc[...] = jnp.zeros_like(item_acc)

    def second_pass(t, carry):
        j = lax.rem(me_i + t, n_items)

        @pl.when(t > 0)
        def _():
            theirs = new_low.at[u_share(j)]
            to(theirs, theirs, as_sem.at[j], ar_sem.at[j], "items", j).wait_recv()

        rows_t = jnp.concatenate(
            [
                new_low[pl.ds(pl.multiple_of((j * share_blocks + b) * edge, edge), edge), :].T
                for b in range(share_blocks)
            ],
            axis=1,
        )

        def step(p, c):
            rows = new_low[u_share(j), :]
            weighted = errors(rows, j * share_blocks, p)
            cols = pl.ds(pl.multiple_of(p * span, span), span)
            item_acc[:, cols] += jnp.dot(rows_t, weighted, preferred_element_type=f32)
            return c

        lax.fori_loop(0, pairs, step, 0)
        return carry

    lax.fori_loop(0, n_items, second_pass, 0)
    for b in range(item_blocks):
        tile = item_acc[:, b * edge : (b + 1) * edge].T
        item_sum[b * edge : (b + 1) * edge, :] = tile
        item_send[b * edge : (b + 1) * edge, :] = tile.astype(bf16)

    def send_items(j):
        return to(
            item_send.at[i_share(j)], recv_i.at[me_u],
            is_sem.at[j], ir_sem.at[me_u], "users", j,
        )

    user_peers(lambda j: send_items(j).start())
    loads[5].wait()
    loads[6].wait()

    def add_items(j):
        to(
            item_send.at[i_share(j)], recv_i.at[j], is_sem.at[j], ir_sem.at[j], "users", j
        ).wait_recv()
        item_sum[i_share(me_u), :] += recv_i[j].astype(f32)

    user_peers(add_items)
    item_scale = 1.0 / math.sqrt(user_rows * n_users)
    new, one, two = adam_update(
        itf[...], im1[...], im2[...], item_sum[i_share(me_u), :], item_scale
    )
    itf[...] = new
    im1[...] = one
    im2[...] = two
    for store in stores[3:]:
        store.start()

    user_peers(lambda j: gather(j).wait_send())
    user_peers(lambda j: send_items(j).wait_send())
    item_peers(lambda j: send_share(j).wait_send())
    item_peers(lambda j: spread(j).wait_send())
    for store in stores:
        store.wait()


def hand_out(*refs):
    count = (len(refs) - 1) // 2
    moves = [
        pltpu.make_async_copy(refs[n], refs[count + n], refs[-1].at[n]) for n in range(count)
    ]
    for move in moves:
        move.start()
    for move in moves:
        move.wait()


def on_device(
    n_users, n_items,
    user_factors, user_moment_one, user_moment_two,
    item_factors, item_moment_one, item_moment_two,
    block_slot, block_count, block_values,
):
    values = block_values[0, 0]
    edge = values.shape[-1]
    user_rows, rank = user_factors.shape
    item_share = item_factors.shape[0]
    item_rows = item_share * n_users
    user_share = user_rows // n_items
    slots = (user_rows // edge) * (item_rows // edge)
    place = find_blocks(block_slot[0, 0], block_count[0, 0], slots)
    vm = pltpu.VMEM
    dma = pltpu.SemaphoreType.DMA
    user_out = jax.ShapeDtypeStruct((user_share, rank), f32)
    item_out = jax.ShapeDtypeStruct((item_share, rank), f32)
    anywhere = pl.BlockSpec(memory_space=pl.ANY)
    out_shape = (user_out,) * 3 + (item_out,) * 3
    results = pl.pallas_call(
        functools.partial(kernel, n_users, n_items, edge),
        out_shape=out_shape,
        in_specs=[pl.BlockSpec(memory_space=pltpu.SMEM)] + [anywhere] * 7,
        out_specs=(anywhere,) * 6,
        scratch_shapes=[
            vm(values.shape, bf16),
            vm((user_rows, rank), f32),
            vm((user_share, rank), f32),
            vm((user_share, rank), f32),
            vm((item_share, rank), f32),
            vm((item_share, rank), f32),
            vm((item_share, rank), f32),
            vm((user_rows, rank), bf16),
            vm((item_rows, rank), bf16),
            vm((rank, item_rows), bf16),
            vm((user_share, rank), f32),
            vm((n_items, user_share, rank), bf16),
            vm((n_items, user_share, rank), bf16),
            vm((user_rows, rank), bf16),
            vm((rank, item_rows), f32),
            vm((item_rows, rank), f32),
            vm((item_rows, rank), bf16),
            vm((n_users, item_share, rank), bf16),
            dma((7,)),
            dma((6,)),
            dma((n_users,)),
            dma((n_users,)),
            dma((n_items,)),
            dma((n_items,)),
            dma((n_items,)),
            dma((n_items,)),
            dma((n_users,)),
            dma((n_users,)),
        ],
        compiler_params=pltpu.CompilerParams(
            collective_id=0, has_side_effects=True, vmem_limit_bytes=56 * 2**20
        ),
        name="factorization_step",
    )(
        place, user_factors, user_moment_one, user_moment_two,
        item_factors, item_moment_one, item_moment_two, values,
    )
    return pl.pallas_call(
        hand_out,
        out_shape=out_shape,
        in_specs=[anywhere] * 6,
        out_specs=(anywhere,) * 6,
        scratch_shapes=[dma((6,))],
        name="hand_out",
    )(*results)


def solution(mesh):
    return jax.shard_map(
        functools.partial(on_device, mesh.shape["users"], mesh.shape["items"]),
        mesh=mesh,
        in_specs=(
            P("users", None),
            P("users", None),
            P("users", None),
            P(("items", "users"), None),
            P(("items", "users"), None),
            P(("items", "users"), None),
            P("users", "items", None),
            P("users", "items"),
            P("users", "items", None, None, None),
        ),
        out_specs=(
            P(("users", "items"), None),
            P(("users", "items"), None),
            P(("users", "items"), None),
            P(("items", "users"), None),
            P(("items", "users"), None),
            P(("items", "users"), None),
        ),
        check_vma=False,
    )
```

```python
import functools
import math

import jax
import jax.numpy as jnp
from jax import lax
from jax.experimental import pallas as pl
from jax.experimental.pallas import tpu as pltpu
from jax.sharding import PartitionSpec as P

conf_alpha = 0.5
reg_weight = 0.5
beta_one = 0.9
beta_two = 0.95
learn_rate = 0.1
adam_eps = 1e-08
correction_one = 1.0 - beta_one**11
correction_two = 1.0 - beta_two**11

f32, bf16 = jnp.float32, jnp.bfloat16


def adam_update(parameter, first_moment, second_moment, grad_sum, grad_scale):
    gradient = grad_sum * grad_scale + reg_weight * parameter
    first_new = beta_one * first_moment + (1.0 - beta_one) * gradient
    second_new = beta_two * second_moment + (1.0 - beta_two) * gradient * gradient
    step_size = first_new / correction_one / (jnp.sqrt(second_new / correction_two) + adam_eps)
    return (parameter - learn_rate * step_size, first_new, second_new)


def find_blocks(slot_list, live_count, slots):
    places = jnp.arange(slot_list.shape[0], dtype=jnp.int32)
    here = (slot_list[None, :] == jnp.arange(slots, dtype=jnp.int32)[:, None]) & (
        places < live_count
    )[None, :]
    return jnp.max(jnp.where(here, places[None, :], -1), axis=1)


def kernel(
    n_users, n_items, edge,
    place, uf_hbm, um1_hbm, um2_hbm, if_hbm, im1_hbm, im2_hbm, vals_hbm,
    nu_hbm, nu1_hbm, nu2_hbm, ni_hbm, ni1_hbm, ni2_hbm,
    vals, uf, um1, um2, itf, im1, im2, u_low, panel, item_t,
    new_user, part, out, in_l, in_r, new_low, item_acc, item_sum, item_send, recv_i,
    load_sem, store_sem, gs_sem, gr_sem, us_sem, ul_sem, ur_sem, as_sem, ar_sem, is_sem, ir_sem,
):
    me_u, me_i = lax.axis_index("users"), lax.axis_index("items")
    user_rows, rank = uf.shape
    item_rows = panel.shape[0]
    user_share, item_share = user_rows // n_items, item_rows // n_users
    chunks, item_blocks = user_share // edge, item_rows // edge
    width = math.gcd(item_blocks, 4)
    steps = item_blocks // width
    span = width * edge
    group = math.gcd(n_items, 4)
    group_rows = group * edge

    def u_share(j):
        return pl.ds(pl.multiple_of(j * user_share, user_share), user_share)

    def block(j):
        return pl.ds(pl.multiple_of(j * edge, edge), edge)

    def i_share(j):
        return pl.ds(pl.multiple_of(j * item_share, item_share), item_share)

    def to(src, dst, s_sem, r_sem, axis, j):
        return pltpu.make_async_remote_copy(
            src_ref=src, dst_ref=dst, send_sem=s_sem, recv_sem=r_sem,
            device_id={axis: j}, device_id_type=pl.DeviceIdType.MESH,
        )

    def user_peers(body):
        def step(t, carry):
            body(lax.rem(me_u + t, n_users))
            return carry

        lax.fori_loop(1, n_users, step, 0)

    def item_peers(body):
        def step(t, carry):
            body(lax.rem(me_i + t, n_items))
            return carry

        lax.fori_loop(1, n_items, step, 0)

    own = u_share(me_i)
    loads = [
        pltpu.make_async_copy(src, dst, load_sem.at[n])
        for n, (src, dst) in enumerate(
            (
                (if_hbm, itf), (uf_hbm, uf), (vals_hbm, vals),
                (um1_hbm.at[own], um1), (um2_hbm.at[own], um2),
                (im1_hbm, im1), (im2_hbm, im2),
            )
        )
    ]
    for load in loads:
        load.start()

    barrier = pltpu.get_barrier_semaphore()

    def greet_user(j):
        pl.semaphore_signal(
            barrier, inc=1, device_id={"users": j}, device_id_type=pl.DeviceIdType.MESH
        )

    def greet_item(j):
        pl.semaphore_signal(
            barrier, inc=1, device_id={"items": j}, device_id_type=pl.DeviceIdType.MESH
        )

    user_peers(greet_user)
    item_peers(greet_item)
    loads[0].wait()
    panel[i_share(me_u), :] = itf[...].astype(bf16)
    pl.semaphore_wait(barrier, n_users + n_items - 2)

    def gather(j):
        mine = panel.at[i_share(me_u)]
        return to(mine, mine, gs_sem.at[j], gr_sem.at[me_u], "users", j)

    def gathered(j):
        theirs = panel.at[i_share(j)]
        return to(theirs, theirs, gs_sem.at[j], gr_sem.at[j], "users", j)

    user_peers(lambda j: gather(j).start())
    loads[1].wait()
    for c in range(chunks):
        for j in range(n_items):
            at = (j * chunks + c) * edge
            u_low[c, j * edge : (j + 1) * edge, :] = uf[at : at + edge, :].astype(bf16)
    loads[2].wait()
    user_peers(lambda j: gathered(j).wait_recv())
    for b in range(item_blocks):
        item_t[:, b * edge : (b + 1) * edge] = panel[b * edge : (b + 1) * edge, :].T

    def errors(rows, c, g, p):
        cols = item_t[:, pl.ds(pl.multiple_of(p * span, span), span)]
        predicted = jnp.dot(rows, cols, preferred_element_type=f32)
        strips = []
        for m in range(group):
            user_block = (g * group + m) * chunks + c
            parts = []
            for h in range(width):
                k = place[user_block * item_blocks + p * width + h]
                live = jnp.where(k < 0, 0.0, 1.0).astype(f32)
                y = vals[jnp.maximum(k, 0)].astype(f32)
                pred = predicted[m * edge : (m + 1) * edge, h * edge : (h + 1) * edge]
                parts.append(((live + (conf_alpha * live) * y) * (pred - y)).astype(bf16))
            strips.append(jnp.concatenate(parts, axis=1))
        return jnp.concatenate(strips, axis=0)

    def group_of(g):
        return pl.ds(pl.multiple_of(g * group_rows, group_rows), group_rows)

    def first_pass(c):
        def one_group(g, carry):
            rows = group_of(g)
            part[c, rows, :] = jnp.zeros((group_rows, rank), f32)

            def step(p, carry):
                weighted = errors(u_low[c, rows, :], c, g, p)
                it = panel[pl.ds(pl.multiple_of(p * span, span), span), :]
                part[c, rows, :] += jnp.dot(weighted, it, preferred_element_type=f32)
                return carry

            return lax.fori_loop(0, steps, step, carry)

        lax.fori_loop(0, n_items // group, one_group, 0)

    right, left = lax.rem(me_i + 1, n_items), lax.rem(me_i + n_items - 1, n_items)

    def upward(c, j):
        return to(
            out.at[c, block(j)], in_l.at[c, block(j)], us_sem.at[c, j], ul_sem.at[c, j],
            "items", right,
        )

    def downward(c, j):
        return to(
            out.at[c, block(j)], in_r.at[c, block(j)], us_sem.at[c, j], ur_sem.at[c, j],
            "items", left,
        )

    def add_left(c, j):
        @pl.when(me_i > 0)
        def _():
            upward(c, j).wait_recv()
            part[c, block(j), :] += in_l[c, block(j), :].astype(f32)

    def add_right(c, j):
        @pl.when(me_i < n_items - 1)
        def _():
            downward(c, j).wait_recv()
            part[c, block(j), :] += in_r[c, block(j), :].astype(f32)

    def send_up(c):
        def one(t, carry):
            j = n_items - 1 - t
            add_left(c, j)
            out[c, block(j), :] = part[c, block(j), :].astype(bf16)
            upward(c, j).start()
            return carry

        lax.fori_loop(0, n_items - 1 - me_i, one, 0)

    def send_down(c):
        def one(j, carry):
            add_right(c, j)
            out[c, block(j), :] = part[c, block(j), :].astype(bf16)
            downward(c, j).start()
            return carry

        lax.fori_loop(0, me_i, one, 0)

    def spread(c, j):
        mine = new_low.at[c, block(me_i)]
        return to(mine, mine, as_sem.at[c, j], ar_sem.at[c, me_i], "items", j)

    user_scale = 1.0 / math.sqrt(item_rows * n_items)

    def update_users(c):
        add_left(c, me_i)
        add_right(c, me_i)
        here = block(c)
        new, one, two = adam_update(
            uf[block(me_i * chunks + c), :], um1[here, :], um2[here, :],
            part[c, block(me_i), :], user_scale,
        )
        new_low[c, block(me_i), :] = new.astype(bf16)
        item_peers(lambda j: spread(c, j).start())
        new_user[here, :] = new
        um1[here, :] = one
        um2[here, :] = two

    def second_pass(c):
        def arrived(j):
            theirs = new_low.at[c, block(j)]
            to(theirs, theirs, as_sem.at[c, j], ar_sem.at[c, j], "items", j).wait_recv()

        item_peers(arrived)

        def one_group(g, carry):
            rows_t = jnp.concatenate(
                [new_low[c, block(g * group + m), :].T for m in range(group)], axis=1
            )

            def step(p, carry):
                weighted = errors(new_low[c, group_of(g), :], c, g, p)
                cols = pl.ds(pl.multiple_of(p * span, span), span)
                item_acc[:, cols] += jnp.dot(rows_t, weighted, preferred_element_type=f32)
                return carry

            return lax.fori_loop(0, steps, step, carry)

        lax.fori_loop(0, n_items // group, one_group, 0)

    item_acc[...] = jnp.zeros_like(item_acc)
    loads[3].wait()
    loads[4].wait()
    below, above = me_i, n_items - 1 - me_i
    farthest = jnp.maximum(below, above)

    def stage(s, carry):
        def at(lag, work):
            @pl.when((s >= lag) & (s < lag + chunks))
            def _():
                work(s - lag)

        at(0, first_pass)
        at(below, send_up)
        at(above, send_down)
        at(farthest, update_users)
        at(n_items, second_pass)
        return carry

    lax.fori_loop(0, chunks + n_items, stage, 0)
    stores = [
        pltpu.make_async_copy(src, dst, store_sem.at[n])
        for n, (src, dst) in enumerate(
            (
                (new_user, nu_hbm), (um1, nu1_hbm), (um2, nu2_hbm),
                (itf, ni_hbm), (im1, ni1_hbm), (im2, ni2_hbm),
            )
        )
    ]
    for store in stores[:3]:
        store.start()
    for b in range(item_blocks):
        tile = item_acc[:, b * edge : (b + 1) * edge].T
        item_sum[b * edge : (b + 1) * edge, :] = tile
        item_send[b * edge : (b + 1) * edge, :] = tile.astype(bf16)

    def send_items(j):
        return to(
            item_send.at[i_share(j)], recv_i.at[me_u],
            is_sem.at[j], ir_sem.at[me_u], "users", j,
        )

    user_peers(lambda j: send_items(j).start())
    loads[5].wait()
    loads[6].wait()

    def add_items(j):
        to(
            item_send.at[i_share(j)], recv_i.at[j], is_sem.at[j], ir_sem.at[j], "users", j
        ).wait_recv()
        item_sum[i_share(me_u), :] += recv_i[j].astype(f32)

    user_peers(add_items)
    item_scale = 1.0 / math.sqrt(user_rows * n_users)
    new, one, two = adam_update(
        itf[...], im1[...], im2[...], item_sum[i_share(me_u), :], item_scale
    )
    itf[...] = new
    im1[...] = one
    im2[...] = two
    for store in stores[3:]:
        store.start()

    user_peers(lambda j: gather(j).wait_send())
    user_peers(lambda j: send_items(j).wait_send())


    def sent(c, carry):
        def one(j, carry):
            @pl.when(j != me_i)
            def _():
                upward(c, j).wait_send()
                spread(c, j).wait_send()

            return carry

        return lax.fori_loop(0, n_items, one, carry)

    lax.fori_loop(0, chunks, sent, 0)
    for store in stores:
        store.wait()


def hand_out(*refs):
    load_sem, store_sem = refs[-2:]
    count = (len(refs) - 2) // 3
    sources, targets, held = (refs[n * count : (n + 1) * count] for n in range(3))
    loads = [pltpu.make_async_copy(sources[n], held[n], load_sem.at[n]) for n in range(count)]
    stores = [pltpu.make_async_copy(held[n], targets[n], store_sem.at[n]) for n in range(count)]
    for load in loads:
        load.start()
    for load, store in zip(loads, stores):
        load.wait()
        store.start()
    for store in stores:
        store.wait()


def on_device(
    n_users, n_items,
    user_factors, user_moment_one, user_moment_two,
    item_factors, item_moment_one, item_moment_two,
    block_slot, block_count, block_values,
):
    values = block_values[0, 0]
    edge = values.shape[-1]
    user_rows, rank = user_factors.shape
    item_share = item_factors.shape[0]
    item_rows = item_share * n_users
    user_share = user_rows // n_items
    chunks = user_share // edge
    by_chunk = (chunks, n_items * edge, rank)
    slots = (user_rows // edge) * (item_rows // edge)
    place = find_blocks(block_slot[0, 0], block_count[0, 0], slots)
    vm = pltpu.VMEM
    dma = pltpu.SemaphoreType.DMA
    user_out = jax.ShapeDtypeStruct((user_share, rank), f32)
    item_out = jax.ShapeDtypeStruct((item_share, rank), f32)
    anywhere = pl.BlockSpec(memory_space=pl.ANY)
    out_shape = (user_out,) * 3 + (item_out,) * 3
    results = pl.pallas_call(
        functools.partial(kernel, n_users, n_items, edge),
        out_shape=out_shape,
        in_specs=[pl.BlockSpec(memory_space=pltpu.SMEM)] + [anywhere] * 7,
        out_specs=(anywhere,) * 6,
        scratch_shapes=[
            vm(values.shape, bf16),
            vm((user_rows, rank), f32),
            vm((user_share, rank), f32),
            vm((user_share, rank), f32),
            vm((item_share, rank), f32),
            vm((item_share, rank), f32),
            vm((item_share, rank), f32),
            vm(by_chunk, bf16),
            vm((item_rows, rank), bf16),
            vm((rank, item_rows), bf16),
            vm((user_share, rank), f32),
            vm(by_chunk, f32),
            vm(by_chunk, bf16),
            vm(by_chunk, bf16),
            vm(by_chunk, bf16),
            vm(by_chunk, bf16),
            vm((rank, item_rows), f32),
            vm((item_rows, rank), f32),
            vm((item_rows, rank), bf16),
            vm((n_users, item_share, rank), bf16),
            dma((7,)),
            dma((6,)),
            dma((n_users,)),
            dma((n_users,)),
            dma((chunks, n_items)),
            dma((chunks, n_items)),
            dma((chunks, n_items)),
            dma((chunks, n_items)),
            dma((chunks, n_items)),
            dma((n_users,)),
            dma((n_users,)),
        ],
        compiler_params=pltpu.CompilerParams(
            collective_id=0, has_side_effects=True, vmem_limit_bytes=56 * 2**20
        ),
        name="factorization_step",
    )(
        place, user_factors, user_moment_one, user_moment_two,
        item_factors, item_moment_one, item_moment_two, values,
    )
    return pl.pallas_call(
        hand_out,
        out_shape=out_shape,
        in_specs=[anywhere] * 6,
        out_specs=(anywhere,) * 6,
        scratch_shapes=[vm(o.shape, f32) for o in out_shape] + [dma((6,)), dma((6,))],
        name="hand_out",
    )(*results)


def solution(mesh):
    return jax.shard_map(
        functools.partial(on_device, mesh.shape["users"], mesh.shape["items"]),
        mesh=mesh,
        in_specs=(
            P("users", None),
            P("users", None),
            P("users", None),
            P(("items", "users"), None),
            P(("items", "users"), None),
            P(("items", "users"), None),
            P("users", "items", None),
            P("users", "items"),
            P("users", "items", None, None, None),
        ),
        out_specs=(
            P(("users", "items"), None),
            P(("users", "items"), None),
            P(("users", "items"), None),
            P(("items", "users"), None),
            P(("items", "users"), None),
            P(("items", "users"), None),
        ),
        check_vma=False,
    )
```

```python
import functools
import math

import jax
import jax.numpy as jnp
from jax import lax
from jax.experimental import pallas as pl
from jax.experimental.pallas import tpu as pltpu
from jax.sharding import PartitionSpec as P

conf_alpha = 0.5
reg_weight = 0.5
beta_one = 0.9
beta_two = 0.95
learn_rate = 0.1
adam_eps = 1e-08
correction_one = 1.0 - beta_one**11
correction_two = 1.0 - beta_two**11

f32, bf16 = jnp.float32, jnp.bfloat16


def adam_update(parameter, first_moment, second_moment, grad_sum, grad_scale):
    gradient = grad_sum * grad_scale + reg_weight * parameter
    first_new = beta_one * first_moment + (1.0 - beta_one) * gradient
    second_new = beta_two * second_moment + (1.0 - beta_two) * gradient * gradient
    step_size = first_new / correction_one / (jnp.sqrt(second_new / correction_two) + adam_eps)
    return (parameter - learn_rate * step_size, first_new, second_new)


def find_blocks(slot_list, live_count, slots):
    places = jnp.arange(slot_list.shape[0], dtype=jnp.int32)
    here = (slot_list[None, :] == jnp.arange(slots, dtype=jnp.int32)[:, None]) & (
        places < live_count
    )[None, :]
    return jnp.max(jnp.where(here, places[None, :], -1), axis=1)


def kernel(
    n_users, n_items, edge,
    place, uf_hbm, um1_hbm, um2_hbm, if_hbm, im1_hbm, im2_hbm, vals_hbm,
    nu_hbm, nu1_hbm, nu2_hbm, ni_hbm, ni1_hbm, ni2_hbm,
    vals, uf, um1, um2, itf, im1, im2, u_low, panel, item_t,
    new_user, part, out, in_l, in_r, new_low, new_t, item_acc, item_sum, item_send, recv_i,
    load_sem, store_sem, gs_sem, gr_sem, us_sem, ul_sem, ur_sem, as_sem, ar_sem, is_sem, ir_sem,
):
    me_u, me_i = lax.axis_index("users"), lax.axis_index("items")
    user_rows, rank = uf.shape
    item_rows = panel.shape[0]
    user_share, item_share = user_rows // n_items, item_rows // n_users
    chunks, item_blocks = user_share // edge, item_rows // edge
    width = math.gcd(item_blocks, 2)
    span = width * edge
    halves = 2 if n_users % 2 == 0 and (item_blocks // width) % 2 == 0 else 1
    steps = item_blocks // width // halves
    half_shares, half_blocks = n_users // halves, item_blocks // halves
    group = math.gcd(n_items, 4)
    group_rows = group * edge

    def u_share(j):
        return pl.ds(pl.multiple_of(j * user_share, user_share), user_share)

    def block(j):
        return pl.ds(pl.multiple_of(j * edge, edge), edge)

    def i_share(j):
        return pl.ds(pl.multiple_of(j * item_share, item_share), item_share)

    def to(src, dst, s_sem, r_sem, axis, j):
        return pltpu.make_async_remote_copy(
            src_ref=src, dst_ref=dst, send_sem=s_sem, recv_sem=r_sem,
            device_id={axis: j}, device_id_type=pl.DeviceIdType.MESH,
        )

    def user_peers(body):
        def step(t, carry):
            body(lax.rem(me_u + t, n_users))
            return carry

        lax.fori_loop(1, n_users, step, 0)

    def item_peers(body):
        def step(t, carry):
            body(lax.rem(me_i + t, n_items))
            return carry

        lax.fori_loop(1, n_items, step, 0)

    own = u_share(me_i)
    loads = [
        pltpu.make_async_copy(src, dst, load_sem.at[n])
        for n, (src, dst) in enumerate(
            (
                (if_hbm, itf), (uf_hbm, uf), (vals_hbm, vals),
                (um1_hbm.at[own], um1), (um2_hbm.at[own], um2),
                (im1_hbm, im1), (im2_hbm, im2),
            )
        )
    ]
    for load in loads:
        load.start()

    barrier = pltpu.get_barrier_semaphore()

    def greet_user(j):
        pl.semaphore_signal(
            barrier, inc=1, device_id={"users": j}, device_id_type=pl.DeviceIdType.MESH
        )

    def greet_item(j):
        pl.semaphore_signal(
            barrier, inc=1, device_id={"items": j}, device_id_type=pl.DeviceIdType.MESH
        )

    user_peers(greet_user)
    item_peers(greet_item)
    loads[0].wait()
    panel[i_share(me_u), :] = itf[...].astype(bf16)
    pl.semaphore_wait(barrier, n_users + n_items - 2)

    def gather(j):
        mine = panel.at[i_share(me_u)]
        return to(mine, mine, gs_sem.at[j], gr_sem.at[me_u], "users", j)

    def gathered(j):
        theirs = panel.at[i_share(j)]
        return to(theirs, theirs, gs_sem.at[j], gr_sem.at[j], "users", j)

    user_peers(lambda j: gather(j).start())
    loads[1].wait()
    for c in range(chunks):
        for j in range(n_items):
            at = (j * chunks + c) * edge
            u_low[c, j * edge : (j + 1) * edge, :] = uf[at : at + edge, :].astype(bf16)
    loads[2].wait()
    user_peers(lambda j: gathered(j).wait_recv())
    for b in range(item_blocks):
        item_t[:, b * edge : (b + 1) * edge] = panel[b * edge : (b + 1) * edge, :].T

    def span_of(p):
        return pl.ds(pl.multiple_of(p * span, span), span)

    def predict(rows, p):
        return jnp.dot(rows, item_t[:, span_of(p)], preferred_element_type=f32)

    def errors(predicted, c, g, p):
        strips = []
        for m in range(group):
            user_block = (g * group + m) * chunks + c
            parts = []
            for h in range(width):
                k = place[user_block * item_blocks + p * width + h]
                live = jnp.where(k < 0, 0.0, 1.0).astype(f32)
                y = vals[jnp.maximum(k, 0)].astype(f32)
                pred = predicted[m * edge : (m + 1) * edge, h * edge : (h + 1) * edge]
                parts.append(((live + (conf_alpha * live) * y) * (pred - y)).astype(bf16))
            strips.append(jnp.concatenate(parts, axis=1))
        return jnp.concatenate(strips, axis=0)

    def sweep(rows, c, g, half, use):
        first = half * steps
        ahead = predict(rows, first)
        for q in range(steps):
            predicted = ahead
            if q < steps - 1:
                ahead = predict(rows, first + q + 1)
            use(errors(predicted, c, g, first + q), first + q)

    def group_of(g):
        return pl.ds(pl.multiple_of(g * group_rows, group_rows), group_rows)

    def first_pass(c):
        def one_group(g, carry):
            rows = group_of(g)
            part[c, rows, :] = jnp.zeros((group_rows, rank), f32)

            def one_half(half, carry):
                def use(weighted, p):
                    part[c, rows, :] += jnp.dot(
                        weighted, panel[span_of(p), :], preferred_element_type=f32
                    )

                sweep(u_low[c, rows, :], c, g, half, use)
                return carry

            return lax.fori_loop(0, halves, one_half, carry)

        lax.fori_loop(0, n_items // group, one_group, 0)

    right, left = lax.rem(me_i + 1, n_items), lax.rem(me_i + n_items - 1, n_items)

    def upward(c, j):
        return to(
            out.at[c, block(j)], in_l.at[c, block(j)], us_sem.at[c, j], ul_sem.at[c, j],
            "items", right,
        )

    def downward(c, j):
        return to(
            out.at[c, block(j)], in_r.at[c, block(j)], us_sem.at[c, j], ur_sem.at[c, j],
            "items", left,
        )

    def add_left(c, j):
        @pl.when(me_i > 0)
        def _():
            upward(c, j).wait_recv()
            part[c, block(j), :] += in_l[c, block(j), :].astype(f32)

    def add_right(c, j):
        @pl.when(me_i < n_items - 1)
        def _():
            downward(c, j).wait_recv()
            part[c, block(j), :] += in_r[c, block(j), :].astype(f32)

    def send_up(c):
        def one(t, carry):
            j = n_items - 1 - t
            add_left(c, j)
            out[c, block(j), :] = part[c, block(j), :].astype(bf16)
            upward(c, j).start()
            return carry

        lax.fori_loop(0, n_items - 1 - me_i, one, 0)

    def send_down(c):
        def one(j, carry):
            add_right(c, j)
            out[c, block(j), :] = part[c, block(j), :].astype(bf16)
            downward(c, j).start()
            return carry

        lax.fori_loop(0, me_i, one, 0)

    def spread(c, j):
        mine = new_low.at[c, block(me_i)]
        return to(mine, mine, as_sem.at[c, j], ar_sem.at[c, me_i], "items", j)

    user_scale = 1.0 / math.sqrt(item_rows * n_items)

    def update_users(c):
        add_left(c, me_i)
        add_right(c, me_i)
        here = block(c)
        new, one, two = adam_update(
            uf[block(me_i * chunks + c), :], um1[here, :], um2[here, :],
            part[c, block(me_i), :], user_scale,
        )
        new_low[c, block(me_i), :] = new.astype(bf16)
        item_peers(lambda j: spread(c, j).start())
        new_user[here, :] = new
        um1[here, :] = one
        um2[here, :] = two

    def second_pass(c):
        def arrived(j):
            theirs = new_low.at[c, block(j)]
            to(theirs, theirs, as_sem.at[c, j], ar_sem.at[c, j], "items", j).wait_recv()

        item_peers(arrived)

        for j in range(n_items):
            new_t[:, j * edge : (j + 1) * edge] = new_low[c, j * edge : (j + 1) * edge, :].T

        def one_half(t, carry):
            half = lax.rem(me_u // half_shares + 1 + t, halves)

            def one_group(g, carry):
                rows_t = new_t[:, group_of(g)]

                def use(weighted, p):
                    item_acc[:, span_of(p)] += jnp.dot(
                        rows_t, weighted, preferred_element_type=f32
                    )

                sweep(new_low[c, group_of(g), :], c, g, half, use)
                return carry

            lax.fori_loop(0, n_items // group, one_group, 0)

            @pl.when(c == chunks - 1)
            def _():
                send_half(half)

            return carry

        lax.fori_loop(0, halves, one_half, 0)

    def send_items(j):
        return to(
            item_send.at[i_share(j)], recv_i.at[me_u],
            is_sem.at[j], ir_sem.at[me_u], "users", j,
        )

    def send_half(half):
        for b in range(half_blocks):
            at = block(half * half_blocks + b)
            tile = item_acc[:, at].T
            item_sum[at, :] = tile
            item_send[at, :] = tile.astype(bf16)

        def one(t, carry):
            j = half * half_shares + lax.rem(me_u + 1 + t, half_shares)

            @pl.when(j != me_u)
            def _():
                send_items(j).start()

            return carry

        lax.fori_loop(0, half_shares, one, 0)

    item_acc[...] = jnp.zeros_like(item_acc)
    loads[3].wait()
    loads[4].wait()
    below, above = me_i, n_items - 1 - me_i
    farthest = jnp.maximum(below, above)

    def stage(s, carry):
        def at(lag, work):
            @pl.when((s >= lag) & (s < lag + chunks))
            def _():
                work(s - lag)

        at(0, first_pass)
        at(below, send_up)
        at(above, send_down)
        at(farthest, update_users)
        at(n_items, second_pass)
        return carry

    lax.fori_loop(0, chunks + n_items, stage, 0)
    stores = [
        pltpu.make_async_copy(src, dst, store_sem.at[n])
        for n, (src, dst) in enumerate(
            (
                (new_user, nu_hbm), (um1, nu1_hbm), (um2, nu2_hbm),
                (itf, ni_hbm), (im1, ni1_hbm), (im2, ni2_hbm),
            )
        )
    ]
    for store in stores[:3]:
        store.start()
    loads[5].wait()
    loads[6].wait()

    def add_items(j):
        to(
            item_send.at[i_share(j)], recv_i.at[j], is_sem.at[j], ir_sem.at[j], "users", j
        ).wait_recv()
        item_sum[i_share(me_u), :] += recv_i[j].astype(f32)

    user_peers(add_items)
    item_scale = 1.0 / math.sqrt(user_rows * n_users)
    new, one, two = adam_update(
        itf[...], im1[...], im2[...], item_sum[i_share(me_u), :], item_scale
    )
    itf[...] = new
    im1[...] = one
    im2[...] = two
    for store in stores[3:]:
        store.start()

    user_peers(lambda j: gather(j).wait_send())
    user_peers(lambda j: send_items(j).wait_send())


    def sent(c, carry):
        def one(j, carry):
            @pl.when(j != me_i)
            def _():
                upward(c, j).wait_send()
                spread(c, j).wait_send()

            return carry

        return lax.fori_loop(0, n_items, one, carry)

    lax.fori_loop(0, chunks, sent, 0)
    for store in stores:
        store.wait()


def hand_out(*refs):
    load_sem, store_sem = refs[-2:]
    count = (len(refs) - 2) // 3
    sources, targets, held = (refs[n * count : (n + 1) * count] for n in range(3))
    loads = [pltpu.make_async_copy(sources[n], held[n], load_sem.at[n]) for n in range(count)]
    stores = [pltpu.make_async_copy(held[n], targets[n], store_sem.at[n]) for n in range(count)]
    for load in loads:
        load.start()
    for load, store in zip(loads, stores):
        load.wait()
        store.start()
    for store in stores:
        store.wait()


def on_device(
    n_users, n_items,
    user_factors, user_moment_one, user_moment_two,
    item_factors, item_moment_one, item_moment_two,
    block_slot, block_count, block_values,
):
    values = block_values[0, 0]
    edge = values.shape[-1]
    user_rows, rank = user_factors.shape
    item_share = item_factors.shape[0]
    item_rows = item_share * n_users
    user_share = user_rows // n_items
    chunks = user_share // edge
    by_chunk = (chunks, n_items * edge, rank)
    slots = (user_rows // edge) * (item_rows // edge)
    place = find_blocks(block_slot[0, 0], block_count[0, 0], slots)
    vm = pltpu.VMEM
    dma = pltpu.SemaphoreType.DMA
    user_out = jax.ShapeDtypeStruct((user_share, rank), f32)
    item_out = jax.ShapeDtypeStruct((item_share, rank), f32)
    anywhere = pl.BlockSpec(memory_space=pl.ANY)
    out_shape = (user_out,) * 3 + (item_out,) * 3
    results = pl.pallas_call(
        functools.partial(kernel, n_users, n_items, edge),
        out_shape=out_shape,
        in_specs=[pl.BlockSpec(memory_space=pltpu.SMEM)] + [anywhere] * 7,
        out_specs=(anywhere,) * 6,
        scratch_shapes=[
            vm(values.shape, bf16),
            vm((user_rows, rank), f32),
            vm((user_share, rank), f32),
            vm((user_share, rank), f32),
            vm((item_share, rank), f32),
            vm((item_share, rank), f32),
            vm((item_share, rank), f32),
            vm(by_chunk, bf16),
            vm((item_rows, rank), bf16),
            vm((rank, item_rows), bf16),
            vm((user_share, rank), f32),
            vm(by_chunk, f32),
            vm(by_chunk, bf16),
            vm(by_chunk, bf16),
            vm(by_chunk, bf16),
            vm(by_chunk, bf16),
            vm((rank, n_items * edge), bf16),
            vm((rank, item_rows), f32),
            vm((item_rows, rank), f32),
            vm((item_rows, rank), bf16),
            vm((n_users, item_share, rank), bf16),
            dma((7,)),
            dma((6,)),
            dma((n_users,)),
            dma((n_users,)),
            dma((chunks, n_items)),
            dma((chunks, n_items)),
            dma((chunks, n_items)),
            dma((chunks, n_items)),
            dma((chunks, n_items)),
            dma((n_users,)),
            dma((n_users,)),
        ],
        compiler_params=pltpu.CompilerParams(
            collective_id=0, has_side_effects=True, vmem_limit_bytes=56 * 2**20
        ),
        name="factorization_step",
    )(
        place, user_factors, user_moment_one, user_moment_two,
        item_factors, item_moment_one, item_moment_two, values,
    )
    return pl.pallas_call(
        hand_out,
        out_shape=out_shape,
        in_specs=[anywhere] * 6,
        out_specs=(anywhere,) * 6,
        scratch_shapes=[vm(o.shape, f32) for o in out_shape] + [dma((6,)), dma((6,))],
        name="hand_out",
    )(*results)


def solution(mesh):
    return jax.shard_map(
        functools.partial(on_device, mesh.shape["users"], mesh.shape["items"]),
        mesh=mesh,
        in_specs=(
            P("users", None),
            P("users", None),
            P("users", None),
            P(("items", "users"), None),
            P(("items", "users"), None),
            P(("items", "users"), None),
            P("users", "items", None),
            P("users", "items"),
            P("users", "items", None, None, None),
        ),
        out_specs=(
            P(("users", "items"), None),
            P(("users", "items"), None),
            P(("users", "items"), None),
            P(("items", "users"), None),
            P(("items", "users"), None),
            P(("items", "users"), None),
        ),
        check_vma=False,
    )
```

```python
import functools
import math

import jax
import jax.numpy as jnp
from jax import lax
from jax.experimental import pallas as pl
from jax.experimental.pallas import tpu as pltpu
from jax.sharding import PartitionSpec as P

conf_alpha = 0.5
reg_weight = 0.5
beta_one = 0.9
beta_two = 0.95
learn_rate = 0.1
adam_eps = 1e-08
correction_one = 1.0 - beta_one**11
correction_two = 1.0 - beta_two**11

f32, bf16 = jnp.float32, jnp.bfloat16


def adam_update(parameter, first_moment, second_moment, grad_sum, grad_scale):
    gradient = grad_sum * grad_scale + reg_weight * parameter
    first_new = beta_one * first_moment + (1.0 - beta_one) * gradient
    second_new = beta_two * second_moment + (1.0 - beta_two) * gradient * gradient
    step_size = first_new / correction_one / (jnp.sqrt(second_new / correction_two) + adam_eps)
    return (parameter - learn_rate * step_size, first_new, second_new)


def find_blocks(slot_list, live_count, slots):
    places = jnp.arange(slot_list.shape[0], dtype=jnp.int32)
    here = (slot_list[None, :] == jnp.arange(slots, dtype=jnp.int32)[:, None]) & (
        places < live_count
    )[None, :]
    return jnp.max(jnp.where(here, places[None, :], -1), axis=1)


def kernel(
    n_users, n_items, edge,
    place, uf_hbm, um1_hbm, um2_hbm, if_hbm, im1_hbm, im2_hbm, vals_hbm,
    nu_hbm, nu1_hbm, nu2_hbm, ni_hbm, ni1_hbm, ni2_hbm,
    vals, uf, um1, um2, itf, im1, im2, u_low, panel, item_t,
    new_user, part, out, in_l, in_r, new_low, new_t, item_acc, item_sum, item_send, recv_i,
    load_sem, store_sem, gs_sem, gr_sem, us_sem, ul_sem, ur_sem, au_sem, ad_sem, ar_sem, is_sem, ir_sem,
):
    me_u, me_i = lax.axis_index("users"), lax.axis_index("items")
    user_rows, rank = uf.shape
    item_rows = panel.shape[0]
    user_share, item_share = user_rows // n_items, item_rows // n_users
    chunks, item_blocks = user_share // edge, item_rows // edge
    width = math.gcd(item_blocks, 2)
    span = width * edge
    halves = 2 if n_users % 2 == 0 and (item_blocks // width) % 2 == 0 else 1
    steps = item_blocks // width // halves
    half_shares, half_blocks = n_users // halves, item_blocks // halves
    group = math.gcd(n_items, 4)
    group_rows = group * edge

    def u_share(j):
        return pl.ds(pl.multiple_of(j * user_share, user_share), user_share)

    def block(j):
        return pl.ds(pl.multiple_of(j * edge, edge), edge)

    def i_share(j):
        return pl.ds(pl.multiple_of(j * item_share, item_share), item_share)

    def to(src, dst, s_sem, r_sem, axis, j):
        return pltpu.make_async_remote_copy(
            src_ref=src, dst_ref=dst, send_sem=s_sem, recv_sem=r_sem,
            device_id={axis: j}, device_id_type=pl.DeviceIdType.MESH,
        )

    def user_peers(body):
        def step(t, carry):
            body(lax.rem(me_u + t, n_users))
            return carry

        lax.fori_loop(1, n_users, step, 0)

    def item_peers(body):
        def step(t, carry):
            body(lax.rem(me_i + t, n_items))
            return carry

        lax.fori_loop(1, n_items, step, 0)

    own = u_share(me_i)
    loads = [
        pltpu.make_async_copy(src, dst, load_sem.at[n])
        for n, (src, dst) in enumerate(
            (
                (if_hbm, itf), (uf_hbm, uf), (vals_hbm, vals),
                (um1_hbm.at[own], um1), (um2_hbm.at[own], um2),
                (im1_hbm, im1), (im2_hbm, im2),
            )
        )
    ]
    for load in loads:
        load.start()

    barrier = pltpu.get_barrier_semaphore()

    def greet_user(j):
        pl.semaphore_signal(
            barrier, inc=1, device_id={"users": j}, device_id_type=pl.DeviceIdType.MESH
        )

    def greet_item(j):
        pl.semaphore_signal(
            barrier, inc=1, device_id={"items": j}, device_id_type=pl.DeviceIdType.MESH
        )

    user_peers(greet_user)
    item_peers(greet_item)
    loads[0].wait()
    panel[i_share(me_u), :] = itf[...].astype(bf16)
    pl.semaphore_wait(barrier, n_users + n_items - 2)

    def gather(j):
        mine = panel.at[i_share(me_u)]
        return to(mine, mine, gs_sem.at[j], gr_sem.at[me_u], "users", j)

    def gathered(j):
        theirs = panel.at[i_share(j)]
        return to(theirs, theirs, gs_sem.at[j], gr_sem.at[j], "users", j)

    user_peers(lambda j: gather(j).start())
    loads[1].wait()
    for c in range(chunks):
        for j in range(n_items):
            at = (j * chunks + c) * edge
            u_low[c, j * edge : (j + 1) * edge, :] = uf[at : at + edge, :].astype(bf16)
    loads[2].wait()
    user_peers(lambda j: gathered(j).wait_recv())
    for b in range(item_blocks):
        item_t[:, b * edge : (b + 1) * edge] = panel[b * edge : (b + 1) * edge, :].T

    def span_of(p):
        return pl.ds(pl.multiple_of(p * span, span), span)

    def predict(rows, p):
        return jnp.dot(rows, item_t[:, span_of(p)], preferred_element_type=f32)

    def errors(predicted, c, g, p):
        strips = []
        for m in range(group):
            user_block = (g * group + m) * chunks + c
            parts = []
            for h in range(width):
                k = place[user_block * item_blocks + p * width + h]
                live = jnp.where(k < 0, 0.0, 1.0).astype(f32)
                y = vals[jnp.maximum(k, 0)].astype(f32)
                pred = predicted[m * edge : (m + 1) * edge, h * edge : (h + 1) * edge]
                parts.append(((live + (conf_alpha * live) * y) * (pred - y)).astype(bf16))
            strips.append(jnp.concatenate(parts, axis=1))
        return jnp.concatenate(strips, axis=0)

    def sweep(rows, c, g, half, use):
        first = half * steps
        ahead = predict(rows, first)
        for q in range(steps):
            predicted = ahead
            if q < steps - 1:
                ahead = predict(rows, first + q + 1)
            use(errors(predicted, c, g, first + q), first + q)

    def group_of(g):
        return pl.ds(pl.multiple_of(g * group_rows, group_rows), group_rows)

    def first_pass(c):
        def one_group(g, carry):
            rows = group_of(g)
            part[c, rows, :] = jnp.zeros((group_rows, rank), f32)

            def one_half(half, carry):
                def use(weighted, p):
                    part[c, rows, :] += jnp.dot(
                        weighted, panel[span_of(p), :], preferred_element_type=f32
                    )

                sweep(u_low[c, rows, :], c, g, half, use)
                return carry

            return lax.fori_loop(0, halves, one_half, carry)

        lax.fori_loop(0, n_items // group, one_group, 0)

    right, left = lax.rem(me_i + 1, n_items), lax.rem(me_i + n_items - 1, n_items)

    def upward(c, j):
        return to(
            out.at[c, block(j)], in_l.at[c, block(j)], us_sem.at[c, j], ul_sem.at[c, j],
            "items", right,
        )

    def downward(c, j):
        return to(
            out.at[c, block(j)], in_r.at[c, block(j)], us_sem.at[c, j], ur_sem.at[c, j],
            "items", left,
        )

    def add_left(c, j):
        @pl.when(me_i > 0)
        def _():
            upward(c, j).wait_recv()
            part[c, block(j), :] += in_l[c, block(j), :].astype(f32)

    def add_right(c, j):
        @pl.when(me_i < n_items - 1)
        def _():
            downward(c, j).wait_recv()
            part[c, block(j), :] += in_r[c, block(j), :].astype(f32)

    def send_up(c):
        def one(t, carry):
            j = n_items - 1 - t
            add_left(c, j)
            out[c, block(j), :] = part[c, block(j), :].astype(bf16)
            upward(c, j).start()
            return carry

        lax.fori_loop(0, n_items - 1 - me_i, one, 0)

    def send_down(c):
        def one(j, carry):
            add_right(c, j)
            out[c, block(j), :] = part[c, block(j), :].astype(bf16)
            downward(c, j).start()
            return carry

        lax.fori_loop(0, me_i, one, 0)

    def pass_up(c, j):
        it = new_low.at[c, block(j)]
        return to(it, it, au_sem.at[c, j], ar_sem.at[c, j], "items", right)

    def pass_down(c, j):
        it = new_low.at[c, block(j)]
        return to(it, it, ad_sem.at[c, j], ar_sem.at[c, j], "items", left)

    def pass_on(c, d):
        @pl.when((me_i - d >= 0) & (me_i < n_items - 1))
        def _():
            pass_up(c, me_i - d).wait_recv()
            pass_up(c, me_i - d).start()

        @pl.when((me_i + d < n_items) & (me_i > 0))
        def _():
            pass_down(c, me_i + d).wait_recv()
            pass_down(c, me_i + d).start()

    def pass_on_far(c):
        def one(d, carry):
            pass_on(c, d)
            return carry

        lax.fori_loop(2, n_items, one, 0)

    def pass_on_near(c):
        pass_on(c, 1)

        @pl.when(c == 0)
        def _():
            pass_on_far(c)

    user_scale = 1.0 / math.sqrt(item_rows * n_items)

    def update_users(c):
        add_left(c, me_i)
        add_right(c, me_i)
        here = block(c)
        new, one, two = adam_update(
            uf[block(me_i * chunks + c), :], um1[here, :], um2[here, :],
            part[c, block(me_i), :], user_scale,
        )
        new_low[c, block(me_i), :] = new.astype(bf16)

        @pl.when(me_i < n_items - 1)
        def _():
            pass_up(c, me_i).start()

        @pl.when(me_i > 0)
        def _():
            pass_down(c, me_i).start()

        new_user[here, :] = new
        um1[here, :] = one
        um2[here, :] = two

    def second_pass(c):
        def arrived(j):
            @pl.when((me_i == 0) | (me_i == n_items - 1))
            def _():
                pass_up(c, j).wait_recv()

        item_peers(arrived)

        for j in range(n_items):
            new_t[:, j * edge : (j + 1) * edge] = new_low[c, j * edge : (j + 1) * edge, :].T

        def one_half(t, carry):
            half = lax.rem(me_u // half_shares + 1 + t, halves)

            def one_group(g, carry):
                rows_t = new_t[:, group_of(g)]

                def use(weighted, p):
                    item_acc[:, span_of(p)] += jnp.dot(
                        rows_t, weighted, preferred_element_type=f32
                    )

                sweep(new_low[c, group_of(g), :], c, g, half, use)
                return carry

            lax.fori_loop(0, n_items // group, one_group, 0)

            @pl.when((t == 0) & (c < chunks - 1))
            def _():
                pass_on_far(c + 1)

            @pl.when(c == chunks - 1)
            def _():
                send_half(half)

            return carry

        lax.fori_loop(0, halves, one_half, 0)

    def send_items(j):
        return to(
            item_send.at[i_share(j)], recv_i.at[me_u],
            is_sem.at[j], ir_sem.at[me_u], "users", j,
        )

    def send_half(half):
        for b in range(half_blocks):
            at = block(half * half_blocks + b)
            tile = item_acc[:, at].T
            item_sum[at, :] = tile
            item_send[at, :] = tile.astype(bf16)

        def one(t, carry):
            j = half * half_shares + lax.rem(me_u + 1 + t, half_shares)

            @pl.when(j != me_u)
            def _():
                send_items(j).start()

            return carry

        lax.fori_loop(0, half_shares, one, 0)

    item_acc[...] = jnp.zeros_like(item_acc)
    loads[3].wait()
    loads[4].wait()
    below, above = me_i, n_items - 1 - me_i
    farthest = jnp.maximum(below, above)

    def stage(s, carry):
        def at(lag, work):
            @pl.when((s >= lag) & (s < lag + chunks))
            def _():
                work(s - lag)

        at(0, first_pass)
        at(below, send_up)
        at(above, send_down)
        at(farthest, update_users)
        at(n_items, pass_on_near)
        at(n_items + 1, second_pass)
        return carry

    lax.fori_loop(0, chunks + n_items + 1, stage, 0)
    stores = [
        pltpu.make_async_copy(src, dst, store_sem.at[n])
        for n, (src, dst) in enumerate(
            (
                (new_user, nu_hbm), (um1, nu1_hbm), (um2, nu2_hbm),
                (itf, ni_hbm), (im1, ni1_hbm), (im2, ni2_hbm),
            )
        )
    ]
    for store in stores[:3]:
        store.start()
    loads[5].wait()
    loads[6].wait()

    def add_items(j):
        to(
            item_send.at[i_share(j)], recv_i.at[j], is_sem.at[j], ir_sem.at[j], "users", j
        ).wait_recv()
        item_sum[i_share(me_u), :] += recv_i[j].astype(f32)

    user_peers(add_items)
    item_scale = 1.0 / math.sqrt(user_rows * n_users)
    new, one, two = adam_update(
        itf[...], im1[...], im2[...], item_sum[i_share(me_u), :], item_scale
    )
    itf[...] = new
    im1[...] = one
    im2[...] = two
    for store in stores[3:]:
        store.start()

    user_peers(lambda j: gather(j).wait_send())
    user_peers(lambda j: send_items(j).wait_send())


    def sent(c, carry):
        def one(j, carry):
            @pl.when(j != me_i)
            def _():
                upward(c, j).wait_send()

            @pl.when((j <= me_i) & (me_i < n_items - 1))
            def _():
                pass_up(c, j).wait_send()

            @pl.when((j >= me_i) & (me_i > 0))
            def _():
                pass_down(c, j).wait_send()

            return carry

        return lax.fori_loop(0, n_items, one, carry)

    lax.fori_loop(0, chunks, sent, 0)
    for store in stores:
        store.wait()


def hand_out(*refs):
    load_sem, store_sem = refs[-2:]
    count = (len(refs) - 2) // 3
    sources, targets, held = (refs[n * count : (n + 1) * count] for n in range(3))
    loads = [pltpu.make_async_copy(sources[n], held[n], load_sem.at[n]) for n in range(count)]
    stores = [pltpu.make_async_copy(held[n], targets[n], store_sem.at[n]) for n in range(count)]
    for load in loads:
        load.start()
    for load, store in zip(loads, stores):
        load.wait()
        store.start()
    for store in stores:
        store.wait()


def on_device(
    n_users, n_items,
    user_factors, user_moment_one, user_moment_two,
    item_factors, item_moment_one, item_moment_two,
    block_slot, block_count, block_values,
):
    values = block_values[0, 0]
    edge = values.shape[-1]
    user_rows, rank = user_factors.shape
    item_share = item_factors.shape[0]
    item_rows = item_share * n_users
    user_share = user_rows // n_items
    chunks = user_share // edge
    by_chunk = (chunks, n_items * edge, rank)
    slots = (user_rows // edge) * (item_rows // edge)
    place = find_blocks(block_slot[0, 0], block_count[0, 0], slots)
    vm = pltpu.VMEM
    dma = pltpu.SemaphoreType.DMA
    user_out = jax.ShapeDtypeStruct((user_share, rank), f32)
    item_out = jax.ShapeDtypeStruct((item_share, rank), f32)
    anywhere = pl.BlockSpec(memory_space=pl.ANY)
    out_shape = (user_out,) * 3 + (item_out,) * 3
    results = pl.pallas_call(
        functools.partial(kernel, n_users, n_items, edge),
        out_shape=out_shape,
        in_specs=[pl.BlockSpec(memory_space=pltpu.SMEM)] + [anywhere] * 7,
        out_specs=(anywhere,) * 6,
        scratch_shapes=[
            vm(values.shape, bf16),
            vm((user_rows, rank), f32),
            vm((user_share, rank), f32),
            vm((user_share, rank), f32),
            vm((item_share, rank), f32),
            vm((item_share, rank), f32),
            vm((item_share, rank), f32),
            vm(by_chunk, bf16),
            vm((item_rows, rank), bf16),
            vm((rank, item_rows), bf16),
            vm((user_share, rank), f32),
            vm(by_chunk, f32),
            vm(by_chunk, bf16),
            vm(by_chunk, bf16),
            vm(by_chunk, bf16),
            vm(by_chunk, bf16),
            vm((rank, n_items * edge), bf16),
            vm((rank, item_rows), f32),
            vm((item_rows, rank), f32),
            vm((item_rows, rank), bf16),
            vm((n_users, item_share, rank), bf16),
            dma((7,)),
            dma((6,)),
            dma((n_users,)),
            dma((n_users,)),
            dma((chunks, n_items)),
            dma((chunks, n_items)),
            dma((chunks, n_items)),
            dma((chunks, n_items)),
            dma((chunks, n_items)),
            dma((chunks, n_items)),
            dma((n_users,)),
            dma((n_users,)),
        ],
        compiler_params=pltpu.CompilerParams(
            collective_id=0, has_side_effects=True, vmem_limit_bytes=56 * 2**20
        ),
        name="factorization_step",
    )(
        place, user_factors, user_moment_one, user_moment_two,
        item_factors, item_moment_one, item_moment_two, values,
    )
    return pl.pallas_call(
        hand_out,
        out_shape=out_shape,
        in_specs=[anywhere] * 6,
        out_specs=(anywhere,) * 6,
        scratch_shapes=[vm(o.shape, f32) for o in out_shape] + [dma((6,)), dma((6,))],
        name="hand_out",
    )(*results)


def solution(mesh):
    return jax.shard_map(
        functools.partial(on_device, mesh.shape["users"], mesh.shape["items"]),
        mesh=mesh,
        in_specs=(
            P("users", None),
            P("users", None),
            P("users", None),
            P(("items", "users"), None),
            P(("items", "users"), None),
            P(("items", "users"), None),
            P("users", "items", None),
            P("users", "items"),
            P("users", "items", None, None, None),
        ),
        out_specs=(
            P(("users", "items"), None),
            P(("users", "items"), None),
            P(("users", "items"), None),
            P(("items", "users"), None),
            P(("items", "users"), None),
            P(("items", "users"), None),
        ),
        check_vma=False,
    )
```

```python
import functools
import math

import jax
import jax.numpy as jnp
from jax import lax
from jax.experimental import pallas as pl
from jax.experimental.pallas import tpu as pltpu
from jax.sharding import PartitionSpec as P

conf_alpha = 0.5
reg_weight = 0.5
beta_one = 0.9
beta_two = 0.95
learn_rate = 0.1
adam_eps = 1e-08
correction_one = 1.0 - beta_one**11
correction_two = 1.0 - beta_two**11

f32, bf16 = jnp.float32, jnp.bfloat16


def adam_update(parameter, first_moment, second_moment, grad_sum, grad_scale):
    gradient = grad_sum * grad_scale + reg_weight * parameter
    first_new = beta_one * first_moment + (1.0 - beta_one) * gradient
    second_new = beta_two * second_moment + (1.0 - beta_two) * gradient * gradient
    step_size = first_new / correction_one / (jnp.sqrt(second_new / correction_two) + adam_eps)
    return (parameter - learn_rate * step_size, first_new, second_new)


def find_blocks(slot_list, live_count, slots):
    places = jnp.arange(slot_list.shape[0], dtype=jnp.int32)
    here = (slot_list[None, :] == jnp.arange(slots, dtype=jnp.int32)[:, None]) & (
        places < live_count
    )[None, :]
    return jnp.max(jnp.where(here, places[None, :], -1), axis=1)


def kernel(
    n_users, n_items, edge,
    place, uf_hbm, um1_hbm, um2_hbm, if_hbm, im1_hbm, im2_hbm, vals_hbm,
    nu_hbm, nu1_hbm, nu2_hbm, ni_hbm, ni1_hbm, ni2_hbm,
    vals, uf, um1, um2, itf, im1, im2, u_low, panel, item_t,
    new_user, part, out, taken, new_low, new_t, item_acc, item_sum, item_send, recv_i,
    load_sem, store_sem, gs_sem, gr_sem, us_sem, ur_sem, as_sem, ar_sem, is_sem, ir_sem,
):
    me_u, me_i = lax.axis_index("users"), lax.axis_index("items")
    user_rows, rank = uf.shape
    item_rows = panel.shape[0]
    user_share, item_share = user_rows // n_items, item_rows // n_users
    chunks, item_blocks = user_share // edge, item_rows // edge
    width = math.gcd(item_blocks, 2)
    span = width * edge
    halves = 2 if n_users % 2 == 0 and (item_blocks // width) % 2 == 0 else 1
    steps = item_blocks // width // halves
    half_shares, half_blocks = n_users // halves, item_blocks // halves
    group = math.gcd(n_items, 4)
    group_rows = group * edge

    def u_share(j):
        return pl.ds(pl.multiple_of(j * user_share, user_share), user_share)

    def block(j):
        return pl.ds(pl.multiple_of(j * edge, edge), edge)

    def i_share(j):
        return pl.ds(pl.multiple_of(j * item_share, item_share), item_share)

    def to(src, dst, s_sem, r_sem, axis, j):
        return pltpu.make_async_remote_copy(
            src_ref=src, dst_ref=dst, send_sem=s_sem, recv_sem=r_sem,
            device_id={axis: j}, device_id_type=pl.DeviceIdType.MESH,
        )

    def user_peers(body):
        def step(t, carry):
            body(lax.rem(me_u + t, n_users))
            return carry

        lax.fori_loop(1, n_users, step, 0)

    def item_peers(body):
        def step(t, carry):
            body(lax.rem(me_i + t, n_items))
            return carry

        lax.fori_loop(1, n_items, step, 0)

    own = u_share(me_i)
    loads = [
        pltpu.make_async_copy(src, dst, load_sem.at[n])
        for n, (src, dst) in enumerate(
            (
                (if_hbm, itf), (uf_hbm, uf), (vals_hbm, vals),
                (um1_hbm.at[own], um1), (um2_hbm.at[own], um2),
                (im1_hbm, im1), (im2_hbm, im2),
            )
        )
    ]
    for load in loads:
        load.start()

    barrier = pltpu.get_barrier_semaphore()

    def greet_user(j):
        pl.semaphore_signal(
            barrier, inc=1, device_id={"users": j}, device_id_type=pl.DeviceIdType.MESH
        )

    def greet_item(j):
        pl.semaphore_signal(
            barrier, inc=1, device_id={"items": j}, device_id_type=pl.DeviceIdType.MESH
        )

    user_peers(greet_user)
    item_peers(greet_item)
    loads[0].wait()
    panel[i_share(me_u), :] = itf[...].astype(bf16)
    pl.semaphore_wait(barrier, n_users + n_items - 2)

    def gather(j):
        mine = panel.at[i_share(me_u)]
        return to(mine, mine, gs_sem.at[j], gr_sem.at[me_u], "users", j)

    def gathered(j):
        theirs = panel.at[i_share(j)]
        return to(theirs, theirs, gs_sem.at[j], gr_sem.at[j], "users", j)

    user_peers(lambda j: gather(j).start())
    loads[1].wait()
    for c in range(chunks):
        for j in range(n_items):
            at = (j * chunks + c) * edge
            u_low[c, j * edge : (j + 1) * edge, :] = uf[at : at + edge, :].astype(bf16)
    loads[2].wait()
    user_peers(lambda j: gathered(j).wait_recv())
    for b in range(item_blocks):
        item_t[:, b * edge : (b + 1) * edge] = panel[b * edge : (b + 1) * edge, :].T

    def span_of(p):
        return pl.ds(pl.multiple_of(p * span, span), span)

    def predict(rows, p):
        return jnp.dot(rows, item_t[:, span_of(p)], preferred_element_type=f32)

    def errors(predicted, c, g, p):
        strips = []
        for m in range(group):
            user_block = (g * group + m) * chunks + c
            parts = []
            for h in range(width):
                k = place[user_block * item_blocks + p * width + h]
                live = jnp.where(k < 0, 0.0, 1.0).astype(f32)
                y = vals[jnp.maximum(k, 0)].astype(f32)
                pred = predicted[m * edge : (m + 1) * edge, h * edge : (h + 1) * edge]
                parts.append(((live + (conf_alpha * live) * y) * (pred - y)).astype(bf16))
            strips.append(jnp.concatenate(parts, axis=1))
        return jnp.concatenate(strips, axis=0)

    def sweep(rows, c, g, half, use):
        first = half * steps
        ahead = predict(rows, first)
        for q in range(steps):
            predicted = ahead
            if q < steps - 1:
                ahead = predict(rows, first + q + 1)
            use(errors(predicted, c, g, first + q), first + q)

    def group_of(g):
        return pl.ds(pl.multiple_of(g * group_rows, group_rows), group_rows)

    def first_pass(c):
        def one_group(g, carry):
            rows = group_of(g)
            part[c, rows, :] = jnp.zeros((group_rows, rank), f32)

            def one_half(half, carry):
                def use(weighted, p):
                    part[c, rows, :] += jnp.dot(
                        weighted, panel[span_of(p), :], preferred_element_type=f32
                    )

                sweep(u_low[c, rows, :], c, g, half, use)
                return carry

            return lax.fori_loop(0, halves, one_half, carry)

        lax.fori_loop(0, n_items // group, one_group, 0)

    def send_part(c, j):
        return to(
            out.at[c, block(j)], taken.at[c, block(me_i)], us_sem.at[c, j], ur_sem.at[c, me_i],
            "items", j,
        )

    def send_parts(c):
        def one(j):
            out[c, block(j), :] = part[c, block(j), :].astype(bf16)
            send_part(c, j).start()

        item_peers(one)

    def spread(c, j):
        mine = new_low.at[c, block(me_i)]
        return to(mine, mine, as_sem.at[c, j], ar_sem.at[c, me_i], "items", j)

    user_scale = 1.0 / math.sqrt(item_rows * n_items)

    def update_users(c):
        def add_part(j):
            to(
                out.at[c, block(j)], taken.at[c, block(j)], us_sem.at[c, j], ur_sem.at[c, j],
                "items", j,
            ).wait_recv()
            part[c, block(me_i), :] += taken[c, block(j), :].astype(f32)

        item_peers(add_part)
        here = block(c)
        new, one, two = adam_update(
            uf[block(me_i * chunks + c), :], um1[here, :], um2[here, :],
            part[c, block(me_i), :], user_scale,
        )
        new_low[c, block(me_i), :] = new.astype(bf16)
        item_peers(lambda j: spread(c, j).start())
        new_user[here, :] = new
        um1[here, :] = one
        um2[here, :] = two

    def second_pass(c):
        def arrived(j):
            theirs = new_low.at[c, block(j)]
            to(theirs, theirs, as_sem.at[c, j], ar_sem.at[c, j], "items", j).wait_recv()

        item_peers(arrived)

        for j in range(n_items):
            new_t[:, j * edge : (j + 1) * edge] = new_low[c, j * edge : (j + 1) * edge, :].T

        def one_half(t, carry):
            half = lax.rem(me_u // half_shares + 1 + t, halves)

            def one_group(g, carry):
                rows_t = new_t[:, group_of(g)]

                def use(weighted, p):
                    item_acc[:, span_of(p)] += jnp.dot(
                        rows_t, weighted, preferred_element_type=f32
                    )

                sweep(new_low[c, group_of(g), :], c, g, half, use)
                return carry

            lax.fori_loop(0, n_items // group, one_group, 0)

            @pl.when(c == chunks - 1)
            def _():
                send_half(half)

            return carry

        lax.fori_loop(0, halves, one_half, 0)

    def send_items(j):
        return to(
            item_send.at[i_share(j)], recv_i.at[me_u],
            is_sem.at[j], ir_sem.at[me_u], "users", j,
        )

    def send_half(half):
        for b in range(half_blocks):
            at = block(half * half_blocks + b)
            tile = item_acc[:, at].T
            item_sum[at, :] = tile
            item_send[at, :] = tile.astype(bf16)

        def one(t, carry):
            j = half * half_shares + lax.rem(me_u + 1 + t, half_shares)

            @pl.when(j != me_u)
            def _():
                send_items(j).start()

            return carry

        lax.fori_loop(0, half_shares, one, 0)

    item_acc[...] = jnp.zeros_like(item_acc)
    loads[3].wait()
    loads[4].wait()

    def stage(s, carry):
        def at(lag, work):
            @pl.when((s >= lag) & (s < lag + chunks))
            def _():
                work(s - lag)

        at(0, first_pass)
        at(0, send_parts)
        at(1, update_users)
        at(3, second_pass)
        return carry

    lax.fori_loop(0, chunks + 3, stage, 0)
    stores = [
        pltpu.make_async_copy(src, dst, store_sem.at[n])
        for n, (src, dst) in enumerate(
            (
                (new_user, nu_hbm), (um1, nu1_hbm), (um2, nu2_hbm),
                (itf, ni_hbm), (im1, ni1_hbm), (im2, ni2_hbm),
            )
        )
    ]
    for store in stores[:3]:
        store.start()
    loads[5].wait()
    loads[6].wait()

    def add_items(j):
        to(
            item_send.at[i_share(j)], recv_i.at[j], is_sem.at[j], ir_sem.at[j], "users", j
        ).wait_recv()
        item_sum[i_share(me_u), :] += recv_i[j].astype(f32)

    user_peers(add_items)
    item_scale = 1.0 / math.sqrt(user_rows * n_users)
    new, one, two = adam_update(
        itf[...], im1[...], im2[...], item_sum[i_share(me_u), :], item_scale
    )
    itf[...] = new
    im1[...] = one
    im2[...] = two
    for store in stores[3:]:
        store.start()

    user_peers(lambda j: gather(j).wait_send())
    user_peers(lambda j: send_items(j).wait_send())


    def sent(c, carry):
        def one(j, carry):
            @pl.when(j != me_i)
            def _():
                send_part(c, j).wait_send()
                spread(c, j).wait_send()

            return carry

        return lax.fori_loop(0, n_items, one, carry)

    lax.fori_loop(0, chunks, sent, 0)
    for store in stores:
        store.wait()


def hand_out(*refs):
    load_sem, store_sem = refs[-2:]
    count = (len(refs) - 2) // 3
    sources, targets, held = (refs[n * count : (n + 1) * count] for n in range(3))
    loads = [pltpu.make_async_copy(sources[n], held[n], load_sem.at[n]) for n in range(count)]
    stores = [pltpu.make_async_copy(held[n], targets[n], store_sem.at[n]) for n in range(count)]
    for load in loads:
        load.start()
    for load, store in zip(loads, stores):
        load.wait()
        store.start()
    for store in stores:
        store.wait()


def on_device(
    n_users, n_items,
    user_factors, user_moment_one, user_moment_two,
    item_factors, item_moment_one, item_moment_two,
    block_slot, block_count, block_values,
):
    values = block_values[0, 0]
    edge = values.shape[-1]
    user_rows, rank = user_factors.shape
    item_share = item_factors.shape[0]
    item_rows = item_share * n_users
    user_share = user_rows // n_items
    chunks = user_share // edge
    by_chunk = (chunks, n_items * edge, rank)
    slots = (user_rows // edge) * (item_rows // edge)
    place = find_blocks(block_slot[0, 0], block_count[0, 0], slots)
    vm = pltpu.VMEM
    dma = pltpu.SemaphoreType.DMA
    user_out = jax.ShapeDtypeStruct((user_share, rank), f32)
    item_out = jax.ShapeDtypeStruct((item_share, rank), f32)
    anywhere = pl.BlockSpec(memory_space=pl.ANY)
    out_shape = (user_out,) * 3 + (item_out,) * 3
    results = pl.pallas_call(
        functools.partial(kernel, n_users, n_items, edge),
        out_shape=out_shape,
        in_specs=[pl.BlockSpec(memory_space=pltpu.SMEM)] + [anywhere] * 7,
        out_specs=(anywhere,) * 6,
        scratch_shapes=[
            vm(values.shape, bf16),
            vm((user_rows, rank), f32),
            vm((user_share, rank), f32),
            vm((user_share, rank), f32),
            vm((item_share, rank), f32),
            vm((item_share, rank), f32),
            vm((item_share, rank), f32),
            vm(by_chunk, bf16),
            vm((item_rows, rank), bf16),
            vm((rank, item_rows), bf16),
            vm((user_share, rank), f32),
            vm(by_chunk, f32),
            vm(by_chunk, bf16),
            vm(by_chunk, bf16),
            vm(by_chunk, bf16),
            vm((rank, n_items * edge), bf16),
            vm((rank, item_rows), f32),
            vm((item_rows, rank), f32),
            vm((item_rows, rank), bf16),
            vm((n_users, item_share, rank), bf16),
            dma((7,)),
            dma((6,)),
            dma((n_users,)),
            dma((n_users,)),
            dma((chunks, n_items)),
            dma((chunks, n_items)),
            dma((chunks, n_items)),
            dma((chunks, n_items)),
            dma((n_users,)),
            dma((n_users,)),
        ],
        compiler_params=pltpu.CompilerParams(
            collective_id=0, has_side_effects=True, vmem_limit_bytes=56 * 2**20
        ),
        name="factorization_step",
    )(
        place, user_factors, user_moment_one, user_moment_two,
        item_factors, item_moment_one, item_moment_two, values,
    )
    return pl.pallas_call(
        hand_out,
        out_shape=out_shape,
        in_specs=[anywhere] * 6,
        out_specs=(anywhere,) * 6,
        scratch_shapes=[vm(o.shape, f32) for o in out_shape] + [dma((6,)), dma((6,))],
        name="hand_out",
    )(*results)


def solution(mesh):
    return jax.shard_map(
        functools.partial(on_device, mesh.shape["users"], mesh.shape["items"]),
        mesh=mesh,
        in_specs=(
            P("users", None),
            P("users", None),
            P("users", None),
            P(("items", "users"), None),
            P(("items", "users"), None),
            P(("items", "users"), None),
            P("users", "items", None),
            P("users", "items"),
            P("users", "items", None, None, None),
        ),
        out_specs=(
            P(("users", "items"), None),
            P(("users", "items"), None),
            P(("users", "items"), None),
            P(("items", "users"), None),
            P(("items", "users"), None),
            P(("items", "users"), None),
        ),
        check_vma=False,
    )
```

```python
import functools
import math

import jax
import jax.numpy as jnp
from jax import lax
from jax.experimental import pallas as pl
from jax.experimental.pallas import tpu as pltpu
from jax.sharding import PartitionSpec as P

conf_alpha = 0.5
reg_weight = 0.5
beta_one = 0.9
beta_two = 0.95
learn_rate = 0.1
adam_eps = 1e-08
correction_one = 1.0 - beta_one**11
correction_two = 1.0 - beta_two**11

f32, bf16 = jnp.float32, jnp.bfloat16


def adam_update(parameter, first_moment, second_moment, grad_sum, grad_scale):
    gradient = grad_sum * grad_scale + reg_weight * parameter
    first_new = beta_one * first_moment + (1.0 - beta_one) * gradient
    second_new = beta_two * second_moment + (1.0 - beta_two) * gradient * gradient
    step_size = first_new / correction_one / (jnp.sqrt(second_new / correction_two) + adam_eps)
    return (parameter - learn_rate * step_size, first_new, second_new)


def find_blocks(slot_list, live_count, slots):
    places = jnp.arange(slot_list.shape[0], dtype=jnp.int32)
    here = (slot_list[None, :] == jnp.arange(slots, dtype=jnp.int32)[:, None]) & (
        places < live_count
    )[None, :]
    return jnp.max(jnp.where(here, places[None, :], -1), axis=1)


def kernel(
    n_users, n_items, edge,
    place, uf_hbm, um1_hbm, um2_hbm, if_hbm, im1_hbm, im2_hbm, vals_hbm,
    nu_hbm, nu1_hbm, nu2_hbm, ni_hbm, ni1_hbm, ni2_hbm,
    vals, uf, um1, um2, itf, im1, im2, u_low, panel, item_t,
    new_user, part, out, taken, new_low, new_t, item_acc, item_sum, item_send, recv_i,
    load_sem, value_sem, store_sem, gs_sem, gr_sem, us_sem, ur_sem, as_sem, ar_sem, is_sem, ir_sem,
):
    me_u, me_i = lax.axis_index("users"), lax.axis_index("items")
    user_rows, rank = uf.shape
    item_rows = panel.shape[0]
    user_share, item_share = user_rows // n_items, item_rows // n_users
    chunks, item_blocks = user_share // edge, item_rows // edge
    width = math.gcd(item_blocks, 2)
    span = width * edge
    halves = 2 if n_users % 2 == 0 and (item_blocks // width) % 2 == 0 else 1
    steps = item_blocks // width // halves
    half_shares, half_blocks = n_users // halves, item_blocks // halves
    group = math.gcd(n_items, 4)
    group_rows = group * edge

    def u_share(j):
        return pl.ds(pl.multiple_of(j * user_share, user_share), user_share)

    def block(j):
        return pl.ds(pl.multiple_of(j * edge, edge), edge)

    def i_share(j):
        return pl.ds(pl.multiple_of(j * item_share, item_share), item_share)

    def to(src, dst, s_sem, r_sem, axis, j):
        return pltpu.make_async_remote_copy(
            src_ref=src, dst_ref=dst, send_sem=s_sem, recv_sem=r_sem,
            device_id={axis: j}, device_id_type=pl.DeviceIdType.MESH,
        )

    def user_peers(body):
        def step(t, carry):
            body(lax.rem(me_u + t, n_users))
            return carry

        lax.fori_loop(1, n_users, step, 0)

    def item_peers(body):
        def step(t, carry):
            body(lax.rem(me_i + t, n_items))
            return carry

        lax.fori_loop(1, n_items, step, 0)

    own = u_share(me_i)
    loads = [
        pltpu.make_async_copy(src, dst, load_sem.at[n])
        for n, (src, dst) in enumerate(
            (
                (if_hbm, itf), (uf_hbm, uf), (im1_hbm, im1),
                (um1_hbm.at[own], um1), (um2_hbm.at[own], um2),
                (im2_hbm, im2),
            )
        )
    ]
    pieces = math.gcd(vals.shape[0], 16)
    piece = vals.shape[0] // pieces
    value_loads = [
        pltpu.make_async_copy(
            vals_hbm.at[n * piece : (n + 1) * piece],
            vals.at[n * piece : (n + 1) * piece],
            value_sem.at[n],
        )
        for n in range(pieces)
    ]
    for load in loads[:2] + value_loads + loads[2:]:
        load.start()

    barrier = pltpu.get_barrier_semaphore()

    def greet_user(j):
        pl.semaphore_signal(
            barrier, inc=1, device_id={"users": j}, device_id_type=pl.DeviceIdType.MESH
        )

    def greet_item(j):
        pl.semaphore_signal(
            barrier, inc=1, device_id={"items": j}, device_id_type=pl.DeviceIdType.MESH
        )

    user_peers(greet_user)
    item_peers(greet_item)
    loads[0].wait()
    panel[i_share(me_u), :] = itf[...].astype(bf16)
    pl.semaphore_wait(barrier, n_users + n_items - 2)

    def gather(j):
        mine = panel.at[i_share(me_u)]
        return to(mine, mine, gs_sem.at[j], gr_sem.at[me_u], "users", j)

    def gathered(j):
        theirs = panel.at[i_share(j)]
        return to(theirs, theirs, gs_sem.at[j], gr_sem.at[j], "users", j)

    user_peers(lambda j: gather(j).start())
    loads[1].wait()
    for c in range(chunks):
        for j in range(n_items):
            at = (j * chunks + c) * edge
            u_low[c, j * edge : (j + 1) * edge, :] = uf[at : at + edge, :].astype(bf16)
    user_peers(lambda j: gathered(j).wait_recv())
    for b in range(item_blocks):
        item_t[:, b * edge : (b + 1) * edge] = panel[b * edge : (b + 1) * edge, :].T
    for load in value_loads:
        load.wait()

    def span_of(p):
        return pl.ds(pl.multiple_of(p * span, span), span)

    def predict(rows, p):
        return jnp.dot(rows, item_t[:, span_of(p)], preferred_element_type=f32)

    def errors(predicted, c, g, p):
        strips = []
        for m in range(group):
            user_block = (g * group + m) * chunks + c
            parts = []
            for h in range(width):
                k = place[user_block * item_blocks + p * width + h]
                live = jnp.where(k < 0, 0.0, 1.0).astype(f32)
                y = vals[jnp.maximum(k, 0)].astype(f32)
                pred = predicted[m * edge : (m + 1) * edge, h * edge : (h + 1) * edge]
                parts.append(((live + (conf_alpha * live) * y) * (pred - y)).astype(bf16))
            strips.append(jnp.concatenate(parts, axis=1))
        return jnp.concatenate(strips, axis=0)

    def sweep(rows, c, g, half, use):
        first = half * steps
        ahead = predict(rows, first)
        for q in range(steps):
            predicted = ahead
            if q < steps - 1:
                ahead = predict(rows, first + q + 1)
            use(errors(predicted, c, g, first + q), first + q)

    def group_of(g):
        return pl.ds(pl.multiple_of(g * group_rows, group_rows), group_rows)

    def first_pass(c):
        def one_group(g, carry):
            rows = group_of(g)
            part[c, rows, :] = jnp.zeros((group_rows, rank), f32)

            def one_half(half, carry):
                def use(weighted, p):
                    part[c, rows, :] += jnp.dot(
                        weighted, panel[span_of(p), :], preferred_element_type=f32
                    )

                sweep(u_low[c, rows, :], c, g, half, use)
                return carry

            return lax.fori_loop(0, halves, one_half, carry)

        lax.fori_loop(0, n_items // group, one_group, 0)

    def send_part(c, j):
        return to(
            out.at[c, block(j)], taken.at[c, block(me_i)], us_sem.at[c, j], ur_sem.at[c, me_i],
            "items", j,
        )

    def send_parts(c):
        def one(j):
            out[c, block(j), :] = part[c, block(j), :].astype(bf16)
            send_part(c, j).start()

        item_peers(one)

    def spread(c, j):
        mine = new_low.at[c, block(me_i)]
        return to(mine, mine, as_sem.at[c, j], ar_sem.at[c, me_i], "items", j)

    user_scale = 1.0 / math.sqrt(item_rows * n_items)

    def update_users(c):
        def add_part(j):
            to(
                out.at[c, block(j)], taken.at[c, block(j)], us_sem.at[c, j], ur_sem.at[c, j],
                "items", j,
            ).wait_recv()
            part[c, block(me_i), :] += taken[c, block(j), :].astype(f32)

        item_peers(add_part)
        here = block(c)
        new, one, two = adam_update(
            uf[block(me_i * chunks + c), :], um1[here, :], um2[here, :],
            part[c, block(me_i), :], user_scale,
        )
        new_low[c, block(me_i), :] = new.astype(bf16)
        item_peers(lambda j: spread(c, j).start())
        new_user[here, :] = new
        um1[here, :] = one
        um2[here, :] = two

    def second_pass(c):
        def arrived(j):
            theirs = new_low.at[c, block(j)]
            to(theirs, theirs, as_sem.at[c, j], ar_sem.at[c, j], "items", j).wait_recv()

        item_peers(arrived)

        for j in range(n_items):
            new_t[:, j * edge : (j + 1) * edge] = new_low[c, j * edge : (j + 1) * edge, :].T

        def one_half(t, carry):
            half = lax.rem(me_u // half_shares + 1 + t, halves)

            def one_group(g, carry):
                rows_t = new_t[:, group_of(g)]

                def use(weighted, p):
                    item_acc[:, span_of(p)] += jnp.dot(
                        rows_t, weighted, preferred_element_type=f32
                    )

                sweep(new_low[c, group_of(g), :], c, g, half, use)
                return carry

            lax.fori_loop(0, n_items // group, one_group, 0)

            @pl.when(c == chunks - 1)
            def _():
                send_half(half)

            return carry

        lax.fori_loop(0, halves, one_half, 0)

    def send_items(j):
        return to(
            item_send.at[i_share(j)], recv_i.at[me_u],
            is_sem.at[j], ir_sem.at[me_u], "users", j,
        )

    def send_half(half):
        for b in range(half_blocks):
            at = block(half * half_blocks + b)
            tile = item_acc[:, at].T
            item_sum[at, :] = tile
            item_send[at, :] = tile.astype(bf16)

        def one(t, carry):
            j = half * half_shares + lax.rem(me_u + 1 + t, half_shares)

            @pl.when(j != me_u)
            def _():
                send_items(j).start()

            return carry

        lax.fori_loop(0, half_shares, one, 0)

    item_acc[...] = jnp.zeros_like(item_acc)
    loads[3].wait()
    loads[4].wait()

    def stage(s, carry):
        def at(lag, work):
            @pl.when((s >= lag) & (s < lag + chunks))
            def _():
                work(s - lag)

        at(0, first_pass)
        at(0, send_parts)
        at(1, update_users)
        at(3, second_pass)
        return carry

    lax.fori_loop(0, chunks + 3, stage, 0)
    stores = [
        pltpu.make_async_copy(src, dst, store_sem.at[n])
        for n, (src, dst) in enumerate(
            (
                (new_user, nu_hbm), (um1, nu1_hbm), (um2, nu2_hbm),
                (itf, ni_hbm), (im1, ni1_hbm), (im2, ni2_hbm),
            )
        )
    ]
    for store in stores[:3]:
        store.start()
    loads[2].wait()
    loads[5].wait()

    def add_items(j):
        to(
            item_send.at[i_share(j)], recv_i.at[j], is_sem.at[j], ir_sem.at[j], "users", j
        ).wait_recv()
        item_sum[i_share(me_u), :] += recv_i[j].astype(f32)

    user_peers(add_items)
    item_scale = 1.0 / math.sqrt(user_rows * n_users)
    new, one, two = adam_update(
        itf[...], im1[...], im2[...], item_sum[i_share(me_u), :], item_scale
    )
    itf[...] = new
    im1[...] = one
    im2[...] = two
    for store in stores[3:]:
        store.start()

    user_peers(lambda j: gather(j).wait_send())
    user_peers(lambda j: send_items(j).wait_send())


    def sent(c, carry):
        def one(j, carry):
            @pl.when(j != me_i)
            def _():
                send_part(c, j).wait_send()
                spread(c, j).wait_send()

            return carry

        return lax.fori_loop(0, n_items, one, carry)

    lax.fori_loop(0, chunks, sent, 0)
    for store in stores:
        store.wait()


def hand_out(*refs):
    load_sem, store_sem = refs[-2:]
    count = (len(refs) - 2) // 3
    sources, targets, held = (refs[n * count : (n + 1) * count] for n in range(3))
    loads = [pltpu.make_async_copy(sources[n], held[n], load_sem.at[n]) for n in range(count)]
    stores = [pltpu.make_async_copy(held[n], targets[n], store_sem.at[n]) for n in range(count)]
    for load in loads:
        load.start()
    for load, store in zip(loads, stores):
        load.wait()
        store.start()
    for store in stores:
        store.wait()


def on_device(
    n_users, n_items,
    user_factors, user_moment_one, user_moment_two,
    item_factors, item_moment_one, item_moment_two,
    block_slot, block_count, block_values,
):
    values = block_values[0, 0]
    edge = values.shape[-1]
    user_rows, rank = user_factors.shape
    item_share = item_factors.shape[0]
    item_rows = item_share * n_users
    user_share = user_rows // n_items
    chunks = user_share // edge
    by_chunk = (chunks, n_items * edge, rank)
    slots = (user_rows // edge) * (item_rows // edge)
    place = find_blocks(block_slot[0, 0], block_count[0, 0], slots)
    vm = pltpu.VMEM
    dma = pltpu.SemaphoreType.DMA
    user_out = jax.ShapeDtypeStruct((user_share, rank), f32)
    item_out = jax.ShapeDtypeStruct((item_share, rank), f32)
    anywhere = pl.BlockSpec(memory_space=pl.ANY)
    out_shape = (user_out,) * 3 + (item_out,) * 3
    results = pl.pallas_call(
        functools.partial(kernel, n_users, n_items, edge),
        out_shape=out_shape,
        in_specs=[pl.BlockSpec(memory_space=pltpu.SMEM)] + [anywhere] * 7,
        out_specs=(anywhere,) * 6,
        scratch_shapes=[
            vm(values.shape, bf16),
            vm((user_rows, rank), f32),
            vm((user_share, rank), f32),
            vm((user_share, rank), f32),
            vm((item_share, rank), f32),
            vm((item_share, rank), f32),
            vm((item_share, rank), f32),
            vm(by_chunk, bf16),
            vm((item_rows, rank), bf16),
            vm((rank, item_rows), bf16),
            vm((user_share, rank), f32),
            vm(by_chunk, f32),
            vm(by_chunk, bf16),
            vm(by_chunk, bf16),
            vm(by_chunk, bf16),
            vm((rank, n_items * edge), bf16),
            vm((rank, item_rows), f32),
            vm((item_rows, rank), f32),
            vm((item_rows, rank), bf16),
            vm((n_users, item_share, rank), bf16),
            dma((6,)),
            dma((math.gcd(values.shape[0], 16),)),
            dma((6,)),
            dma((n_users,)),
            dma((n_users,)),
            dma((chunks, n_items)),
            dma((chunks, n_items)),
            dma((chunks, n_items)),
            dma((chunks, n_items)),
            dma((n_users,)),
            dma((n_users,)),
        ],
        compiler_params=pltpu.CompilerParams(
            collective_id=0, has_side_effects=True, vmem_limit_bytes=56 * 2**20
        ),
        name="factorization_step",
    )(
        place, user_factors, user_moment_one, user_moment_two,
        item_factors, item_moment_one, item_moment_two, values,
    )
    return pl.pallas_call(
        hand_out,
        out_shape=out_shape,
        in_specs=[anywhere] * 6,
        out_specs=(anywhere,) * 6,
        scratch_shapes=[vm(o.shape, f32) for o in out_shape] + [dma((6,)), dma((6,))],
        name="hand_out",
    )(*results)


def solution(mesh):
    return jax.shard_map(
        functools.partial(on_device, mesh.shape["users"], mesh.shape["items"]),
        mesh=mesh,
        in_specs=(
            P("users", None),
            P("users", None),
            P("users", None),
            P(("items", "users"), None),
            P(("items", "users"), None),
            P(("items", "users"), None),
            P("users", "items", None),
            P("users", "items"),
            P("users", "items", None, None, None),
        ),
        out_specs=(
            P(("users", "items"), None),
            P(("users", "items"), None),
            P(("users", "items"), None),
            P(("items", "users"), None),
            P(("items", "users"), None),
            P(("items", "users"), None),
        ),
        check_vma=False,
    )
```
